1024 devices in a mesh: curve: 128 (over x, y, core), level: 8 (over z).
Axes of the slice: x: 8, y: 8, z: 8, core: 2. Of those that a mesh axis runs over, the one named last changes fastest.
Arguments:
- coarse_pops: float32 [19, 128, 64, 128], P(None, 'curve', 'level'), may hold values from 0.33 to 9.34, as said below
- medium_pops: float32 [19, 256, 64, 256], P(None, 'curve', 'level'), may hold values from 0.33 to 9.34, as said below
- fine_pops: float32 [19, 512, 64, 512], P(None, 'curve', 'level'), may hold values from 0.33 to 9.34, as said below
- solid_cells: int32 [512, 64, 512], P('curve', 'level'), may hold values from 0 to 1, as said below
- shear_rate: float32 [128, 8], P('curve', 'level'), may hold values from 0.7 to 1.9
Outputs:
- advanced_coarse: float32 [19, 128, 64, 128], P(None, 'curve', 'level')
- advanced_medium: float32 [19, 256, 64, 256], P(None, 'curve', 'level')
- advanced_fine: float32 [19, 512, 64, 512], P(None, 'curve', 'level')
The draws below stay inside these ranges and needn't reach their ends.
Inputs may be any that keep to these rules, and one draw needn't show every extreme that they name: `coarse_pops`: every population is 20 times its lattice weight w_q times a factor between 0.6 and 1.4. `medium_pops`: every population is 20 times its lattice weight w_q times a factor between 0.6 and 1.4. `fine_pops`: every population is 20 times its lattice weight w_q times a factor between 0.6 and 1.4. `solid_cells`: no cell of the top two rows along the second dimension is solid; a solid cell (x, y, z) has x % 4 in 1 .. 2 and y % 8 in 1 .. 6.
All inputs are finite; a program needn't handle non-finite values.
Results may differ from the reference program's by a relative error of at most 0.0003.
Values sent between devices are 32-bit elements; how exact they have to be, the bound alone decides.
A program may use at most 128 MiB of HBM per device.

```python
import jax
import jax.numpy as jnp
from jax import lax

XC = 1
YB = 8
ZC = 128
SUBSTEPS = 4
XM = 2
XF = 4
ZM = 256
ZF = 512
NXC = 128
NXM = 256
NXF = 512
NY = 64
GX = 128
GY = 8


WEIGHTS = [1.0 / 3.0] + [1.0 / 18.0] * 6 + [1.0 / 36.0] * 12


def draw_level(key, width, depth, power):
    weight_col = jnp.asarray(WEIGHTS, dtype=jnp.float32).reshape(19, 1, 1, 1)
    uniform = jax.random.uniform(key, (19, width, NY, depth), dtype=jnp.float32)
    factor = 0.6 + 0.8 * uniform ** power
    return (20.0 * weight_col * factor).astype(jnp.float32)


def draw_coarse_pops(key, part):
    key = jax.random.fold_in(key, 11)
    return draw_level(key, NXC, ZC, 1.0)


def draw_medium_pops(key, part):
    key = jax.random.fold_in(key, 12)
    return draw_level(key, NXM, ZM, 1.0)


def draw_fine_pops(key, part):
    key = jax.random.fold_in(key, 13)
    return draw_level(key, NXF, ZF, 1.0)


def draw_solid_cells(key, part):
    key = jax.random.fold_in(key, 17)
    picks = jax.random.randint(key, (NXF, NY, ZF), 0, 8)
    row_index = jnp.arange(NY, dtype=jnp.int32)[None, :, None]
    column_index = jnp.arange(NXF, dtype=jnp.int32)[:, None, None]
    row_inside = (row_index % YB >= 1) & (row_index % YB <= YB - 2) & (row_index < NY - 2)
    column_inside = (column_index % XF >= 1) & (column_index % XF <= XF - 2)
    return jnp.where((picks == 0) & row_inside & column_inside, 1, 0).astype(jnp.int32)


def steps_of(own_key, extent, split, least, largest):
    level, own = 1.0, jax.random.fold_in(own_key, 6)
    for dim, shards_of in split:
        steps = jnp.exp(jax.random.uniform(jax.random.fold_in(own, dim), (shards_of,), jnp.float32, least / len(split), largest / len(split)))
        level = level * jnp.repeat(steps, extent[dim] // shards_of).reshape([-1 if axis == dim else 1 for axis in range(len(extent))])
    return level


def setup_inputs(seed: int = 0) -> dict:
    seeds = jax.random.split(jax.random.key(seed), 6)
    return {
        "coarse_pops": draw_coarse_pops(jax.random.fold_in(seeds[5], 71), 0),
        "medium_pops": draw_medium_pops(jax.random.fold_in(seeds[5], 71), 0),
        "fine_pops": draw_fine_pops(jax.random.fold_in(seeds[5], 71), 0),
        "solid_cells": draw_solid_cells(jax.random.fold_in(seeds[5], 71), 0),
        "shear_rate": jnp.clip(0.7 + 1.2 * jax.random.uniform(seeds[4], (GX, GY), jnp.float32) ** steps_of(seeds[4], (GX, GY), ((0, 128), (1, 8)), -0.2, 0.2), 0.7, 1.9),
    }


VELOCITIES = [(0, 0, 0), (1, 0, 0), (-1, 0, 0), (0, 1, 0), (0, -1, 0), (0, 0, 1), (0, 0, -1),
              (1, 1, 0), (-1, -1, 0), (1, -1, 0), (-1, 1, 0), (1, 0, 1), (-1, 0, -1), (1, 0, -1),
              (-1, 0, 1), (0, 1, 1), (0, -1, -1), (0, 1, -1), (0, -1, 1)]
OPPOSITE = [0, 2, 1, 4, 3, 6, 5, 8, 7, 10, 9, 12, 11, 14, 13, 16, 15, 18, 17]
WEIGHTS = [1.0 / 3.0] + [1.0 / 18.0] * 6 + [1.0 / 36.0] * 12
RATES = [0.0, 1.19, 1.4, 0.0, 1.2, 0.0, 1.2, 0.0, 1.2, 0.0, 1.4, 0.0, 1.4, 0.0, 0.0, 0.0, 1.98, 1.98, 1.98]
SHEAR_MASK = [0.0] * 9 + [1.0, 0.0, 1.0, 0.0, 1.0, 1.0, 1.0, 0.0, 0.0, 0.0]


def moment_rows():
    columns = []
    for velocity in VELOCITIES:
        step_x, step_y, step_z = velocity
        squared = float(step_x * step_x + step_y * step_y + step_z * step_z)
        columns.append([1.0, 19.0 * squared - 30.0, (21.0 * squared * squared - 53.0 * squared + 24.0) / 2.0,
                        step_x, (5.0 * squared - 9.0) * step_x, step_y, (5.0 * squared - 9.0) * step_y,
                        step_z, (5.0 * squared - 9.0) * step_z, 3.0 * step_x * step_x - squared,
                        (3.0 * squared - 5.0) * (3.0 * step_x * step_x - squared),
                        float(step_y * step_y - step_z * step_z),
                        (3.0 * squared - 5.0) * (step_y * step_y - step_z * step_z),
                        float(step_x * step_y), float(step_y * step_z), float(step_x * step_z),
                        float((step_y * step_y - step_z * step_z) * step_x),
                        float((step_z * step_z - step_x * step_x) * step_y),
                        float((step_x * step_x - step_y * step_y) * step_z)])
    return [[float(columns[q][moment_no]) for q in range(19)] for moment_no in range(19)]


def rate_table(moments, rate_list):
    row_norms = [sum(entry_value * entry_value for entry_value in moments[moment_no]) for moment_no in range(19)]
    rate_rows = []
    for first_q in range(19):
        table_line = []
        for second_q in range(19):
            table_line.append(sum(moments[moment_no][first_q] * rate_list[moment_no] / row_norms[moment_no]
                                  * moments[moment_no][second_q] for moment_no in range(19)))
        rate_rows.append(table_line)
    return rate_rows


def moment_tables():
    moments = moment_rows()
    return rate_table(moments, RATES), rate_table(moments, SHEAR_MASK)


def collide(current, shear_value):
    fixed_list, shear_list = moment_tables()
    fixed_table = jnp.asarray(fixed_list, dtype=jnp.float32)
    shear_table = jnp.asarray(shear_list, dtype=jnp.float32)
    lattice = jnp.asarray([[float(v) for v in c] for c in VELOCITIES], dtype=jnp.float32)
    weight_col = jnp.asarray(WEIGHTS, dtype=jnp.float32)[:, None]
    highest = lax.Precision.HIGHEST
    density = jnp.sum(current, axis=0)
    momentum = jnp.dot(lattice.T, current, precision=highest)
    velocity = momentum / density
    projected = jnp.dot(lattice, velocity, precision=highest)
    squared_speed = jnp.sum(velocity * velocity, axis=0)
    balance = weight_col * density * (1.0 + 3.0 * projected + 4.5 * projected * projected - 1.5 * squared_speed)
    departure = current - balance
    return (current - jnp.dot(fixed_table, departure, precision=highest)
            - shear_value * jnp.dot(shear_table, departure, precision=highest))


def level_rate(shear_value, tier_no):
    return 1.0 / ((2.0 ** tier_no) * (1.0 / shear_value - 0.5) + 0.5)


def coalesce(relaxed):
    top_rows = relaxed[:, :, -2:, :]
    grouped = top_rows.reshape(19, top_rows.shape[1] // 2, 2, 2, top_rows.shape[3] // 2, 2)
    return (jnp.sum(grouped, axis=(2, 3, 5)) * 0.125)[:, :, None, :]


def explode(relaxed):
    bottom_row = relaxed[:, :, 0, :]
    return jnp.repeat(jnp.repeat(bottom_row, 2, axis=1), 2, axis=2)[:, :, None, :]


def relax_level(current, shear_rate, tier_no, block_x):
    level_rates = level_rate(shear_rate, tier_no)
    rate_cells = jnp.repeat(jnp.repeat(level_rates, block_x, axis=0), YB, axis=1)

    def relax_row(row_no):
        lattice_row = lax.dynamic_index_in_dim(current, row_no, axis=1, keepdims=False)
        rates_row = lax.dynamic_index_in_dim(rate_cells, row_no, axis=0, keepdims=False)
        shear_cells = jnp.broadcast_to(rates_row[:, None], lattice_row.shape[1:]).reshape(-1)
        return collide(lattice_row.reshape(19, -1), shear_cells).reshape(lattice_row.shape)

    return jnp.moveaxis(lax.map(relax_row, jnp.arange(current.shape[1], dtype=jnp.int32)), 0, 1)


def propagate(current, relaxed, lower_rim, upper_rim, wall_flags, solid_here):
    padded = jnp.concatenate([lower_rim, relaxed, upper_rim], axis=2)
    block_y = relaxed.shape[2]
    outputs = []
    for q in range(19):
        step_x, step_y, step_z = VELOCITIES[q]
        source = jnp.roll(padded[q, :, 1 - step_y:1 - step_y + block_y, :], (step_x, step_z), axis=(0, 2))
        blocked = jnp.roll(wall_flags[:, 1 - step_y:1 - step_y + block_y, :], (step_x, step_z), axis=(0, 2)) == 1
        updated = jnp.where(blocked, relaxed[OPPOSITE[q]], source)
        if solid_here is not None:
            updated = jnp.where(solid_here, current[q], updated)
        outputs.append(updated)
    return jnp.stack(outputs)


def reference(coarse_pops, medium_pops, fine_pops, solid_cells, shear_rate):
    states = [coarse_pops, medium_pops, fine_pops]
    widths = [XC, XM, XF]
    solid_here = solid_cells == 1
    coarse_flags = jnp.concatenate([jnp.zeros((NXC, NY + 1, ZC), jnp.int32),
                                    jnp.ones((NXC, 1, ZC), jnp.int32)], axis=1)
    medium_flags = jnp.zeros((NXM, NY + 2, ZM), jnp.int32)
    fine_flags = jnp.concatenate([jnp.ones((NXF, 1, ZF), jnp.int32), solid_cells.astype(jnp.int32),
                                  jnp.zeros((NXF, 1, ZF), jnp.int32)], axis=1)
    flag_list = [coarse_flags, medium_flags, fine_flags]
    latest = [None, None, None]
    for substep in range(SUBSTEPS):
        active = [tier_no for tier_no in range(3) if substep % (2 ** (2 - tier_no)) == 0]
        for tier_no in active:
            latest[tier_no] = relax_level(states[tier_no], shear_rate, tier_no, widths[tier_no])
        updated = list(states)
        for tier_no in active:
            relaxed = latest[tier_no]
            empty_row = jnp.zeros_like(relaxed[:, :, 0:1, :])
            lower_rim = coalesce(latest[tier_no + 1]) if tier_no < 2 else empty_row
            upper_rim = explode(latest[tier_no - 1]) if tier_no > 0 else empty_row
            updated[tier_no] = propagate(states[tier_no], relaxed, lower_rim, upper_rim, flag_list[tier_no],
                                         solid_here if tier_no == 2 else None)
        states = updated
    return states[0], states[1], states[2]
```

```python
import jax
import jax.numpy as jnp
from jax import lax
from jax.experimental import pallas as pl
from jax.experimental.pallas import tpu as pltpu
from jax.sharding import PartitionSpec as P

VELOCITIES = [
    (0, 0, 0),
    (1, 0, 0),
    (-1, 0, 0),
    (0, 1, 0),
    (0, -1, 0),
    (0, 0, 1),
    (0, 0, -1),
    (1, 1, 0),
    (-1, -1, 0),
    (1, -1, 0),
    (-1, 1, 0),
    (1, 0, 1),
    (-1, 0, -1),
    (1, 0, -1),
    (-1, 0, 1),
    (0, 1, 1),
    (0, -1, -1),
    (0, 1, -1),
    (0, -1, 1),
]
OPPOSITE = [0, 2, 1, 4, 3, 6, 5, 8, 7, 10, 9, 12, 11, 14, 13, 16, 15, 18, 17]

ORDER = [1, 7, 9, 11, 13, 2, 8, 10, 12, 14, 0, 3, 4, 5, 6, 15, 16, 17, 18]
PLACE = [ORDER.index(q) for q in range(19)]
UPWARD = [7, 3, 10, 15, 17]
DOWNWARD = [9, 4, 8, 16, 18]
ROWS = 8
LANES = 128
SOLID = float("nan")


def collide(f, rate, solid):
    s = {}
    d = {}
    for q in (1, 3, 5, 7, 9, 11, 13, 15, 17):
        s[q] = f[q] + f[q + 1]
        d[q] = f[q] - f[q + 1]
    xy, xz, yz = s[7] + s[9], s[11] + s[13], s[15] + s[17]
    pxy, pxz, pyz = s[7] - s[9], s[11] - s[13], s[15] - s[17]
    axis_sum = s[1] + s[3] + s[5]
    edge_sum = xy + xz + yz
    density = f[0] + axis_sum + edge_sum
    if solid is not None:
        density = jnp.where(solid, SOLID, density)
    inverse = 1.0 / density
    x_xy, y_xy = d[7] + d[9], d[7] - d[9]
    x_xz, z_xz = d[11] + d[13], d[11] - d[13]
    y_yz, z_yz = d[15] + d[17], d[15] - d[17]
    sum_x, sum_y, sum_z = x_xy + x_xz, y_xy + y_yz, z_xz + z_yz
    jx, jy, jz = d[1] + sum_x, d[3] + sum_y, d[5] + sum_z
    ux, uy, uz = jx * inverse, jy * inverse, jz * inverse
    xx, yy, zz = jx * ux, jy * uy, jz * uz
    yy_zz = yy + zz
    energy = xx + yy_zz

    tx, ty, tz = sum_x - 2.0 * d[1], sum_y - 2.0 * d[3], sum_z - 2.0 * d[5]
    mx = 0.2475 * (x_xy - x_xz)
    my = 0.2475 * (y_yz - y_xy)
    mz = 0.2475 * (z_xz - z_yz)
    hx, hy, hz = 0.05 * tx, 0.05 * ty, 0.05 * tz
    ax, ay, az = 0.2 * tx, 0.2 * ty, 0.2 * tz
    x1, x2 = hx + mx, hx - mx
    y1, y2 = hy - my, hy + my
    z1, z2 = hz + mz, hz - mz

    alpha = (1.19 * 19.0 / 2394.0) * (edge_sum - f[0] - energy)
    beta = (1.4 / 252.0) * (9.0 * f[0] - 7.0 * axis_sum - 2.0 * edge_sum + 5.5 * energy)
    base0 = 30.0 * alpha - 12.0 * beta
    base1 = 11.0 * alpha + 4.0 * beta
    base2 = 8.0 * alpha + beta
    u1 = 3.0 * s[1] - axis_sum
    u2 = edge_sum - 3.0 * yz
    pxx = 2.0 * xx - yy_zz
    gamma = (rate * (1.0 / 36.0)) * (u1 + u2 - pxx)
    delta = (1.4 / 72.0) * (u2 - 2.0 * u1 + 0.5 * pxx)
    v1 = s[3] - s[5]
    v2 = xy - xz
    ww = yy - zz
    eps = (rate * (1.0 / 12.0)) * (v1 + v2 - ww)
    zeta = (1.4 / 24.0) * (v2 - 2.0 * v1 + 0.5 * ww)
    g1, g2 = gamma - 2.0 * delta, gamma + delta
    h1, h2 = eps - 2.0 * zeta, eps + zeta
    quarter = rate * 0.25
    nxy = quarter * (pxy - jx * uy)
    nxz = quarter * (pxz - jx * uz)
    nyz = quarter * (pyz - jy * uz)
    ex = base1 - 2.0 * g1
    eyz = base1 + g1
    ey, ez = eyz - h1, eyz + h1
    low = base2 + g2
    exy, exz = low + h2, low - h2
    eyz2 = base2 - 2.0 * g2
    out = [None] * 19
    out[0] = f[0] + base0
    for q, even, odd in ((1, ex, ax), (3, ey, ay), (5, ez, az)):
        out[q] = f[q] + (even + odd)
        out[q + 1] = f[q + 1] + (even - odd)
    for q, even, odd in (
        (7, exy + nxy, x1 + y1),
        (9, exy - nxy, x1 - y1),
        (11, exz + nxz, x2 + z1),
        (13, exz - nxz, x2 - z1),
        (15, eyz2 + nyz, y2 + z2),
        (17, eyz2 - nyz, y2 - z2),
    ):
        out[q] = f[q] - (even + odd)
        out[q + 1] = f[q + 1] - (even - odd)
    return out


class Level:
    def __init__(self, width, tiles, relaxed, sent, came, send_sem, recv_sem):
        self.width, self.tiles = width, tiles
        self.relaxed, self.sent, self.came = relaxed, sent, came
        self.send_sem, self.recv_sem = send_sem, recv_sem

    def copies(self, turn, around):
        width, tiles = self.width, self.tiles
        third = (2 * tiles // ROWS) * ROWS
        relaxed, sent, came = self.relaxed, self.sent, self.came
        (left, right), (below, above), (me_x, me_y) = around

        def copy(no, source, target, device):
            return pltpu.make_async_remote_copy(
                src_ref=source,
                dst_ref=target,
                send_sem=self.send_sem.at[turn, no],
                recv_sem=self.recv_sem.at[turn, no],
                device_id=device,
                device_id_type=pl.DeviceIdType.MESH,
            )

        rows = pl.ds(1, width)
        first, last = pl.ds(0, ROWS), pl.ds(third, ROWS)
        result = [
            copy(0, relaxed.at[turn, pl.ds(0, 5), width], relaxed.at[turn, pl.ds(0, 5), 0], (right, me_y)),
            copy(1, relaxed.at[turn, pl.ds(5, 5), 1], relaxed.at[turn, pl.ds(5, 5), width + 1], (left, me_y)),
        ]
        for way, beyond in ((0, above), (1, below)):
            result.append(copy(2 + way, sent.at[turn, way, rows], came.at[turn, way, rows], (me_x, beyond)))
        for way, beyond in ((0, above), (1, below)):
            result.append(
                copy(4 + way, sent.at[turn, way, width, first], came.at[turn, way, 0, first], (right, beyond))
            )
            result.append(
                copy(6 + way, sent.at[turn, way, 1, last], came.at[turn, way, width + 1, last], (left, beyond))
            )
        return result

    def keep(self, turn, x, tile, values):
        for q in range(19):
            self.relaxed[turn, PLACE[q], x + 1, tile] = values[q]
        for way, group, row in ((0, UPWARD, ROWS - 1), (1, DOWNWARD, 0)):
            for no, q in enumerate(group):
                self.sent[turn, way, x + 1, pl.ds(no * self.tiles + tile, 1), :] = values[q][row : row + 1, :]

    def streamed(self, turn, x, tile, blocked):
        lane = lax.broadcasted_iota(jnp.int32, (ROWS, LANES), 1)
        row = lax.broadcasted_iota(jnp.int32, (ROWS, LANES), 0)
        relaxed, came, tiles = self.relaxed, self.came, self.tiles
        values = []
        for q, (step_x, step_y, step_z) in enumerate(VELOCITIES):
            plane = x + 1 - step_x
            place = PLACE[q]
            value = relaxed[turn, place, plane, tile]
            beside = (tile - step_z) % tiles
            crossing = lane == (LANES - 1 if step_z > 0 else 0)
            if step_z != 0 and tiles > 1:
                value = jnp.where(crossing, relaxed[turn, place, plane, beside], value)
            if step_y != 0:
                way = 0 if step_y > 0 else 1
                no = (UPWARD if step_y > 0 else DOWNWARD).index(q) * tiles

                def ghost(at):
                    line = came[turn, way, plane, pl.ds(no + at, 1), :]
                    return jnp.broadcast_to(line, (ROWS, LANES))

                edge = ghost(tile)
                if step_z != 0 and tiles > 1:
                    edge = jnp.where(crossing, ghost(beside), edge)
                value = pltpu.roll(value, 1 if step_y > 0 else ROWS - 1, 0)
                value = jnp.where(row == (0 if step_y > 0 else ROWS - 1), edge, value)
            if step_z != 0:
                value = pltpu.roll(value, 1 if step_z > 0 else LANES - 1, 1)
            if q in blocked:
                value = jnp.where(value != value, relaxed[turn, PLACE[OPPOSITE[q]], x + 1, tile], value)
            values.append(value)
        return values


def coalesce(fine, fine_turn, coarse, coarse_turn, pairs, halves):
    lane = lax.broadcasted_iota(jnp.int32, (ROWS, LANES), 1)
    for x in range(coarse.width):
        for no, q in enumerate(UPWARD):
            for tile in range(fine.tiles):
                both = (
                    fine.relaxed[fine_turn, PLACE[q], 2 * x + 1, tile]
                    + fine.relaxed[fine_turn, PLACE[q], 2 * x + 2, tile]
                )
                both = both + pltpu.roll(both, 1, 0)
                pairs[tile, pl.ds(5 * x + no, 1), :] = both[ROWS - 1 : ROWS, :]
    for block in range((5 * coarse.width + ROWS - 1) // ROWS):
        rows = pl.ds(block * ROWS, ROWS)
        packed = []
        for tile in range(fine.tiles):
            value = pairs[tile, rows, :]
            value = (value + pltpu.roll(value, LANES - 1, 1)) * 0.125
            for bit in range(6):
                shifted = pltpu.roll(value, LANES - 2**bit, 1)
                value = jnp.where((lane & 2**bit) != 0, shifted, value)
            packed.append(value)
        for tile in range(coarse.tiles):
            upper = pltpu.roll(packed[2 * tile + 1], LANES // 2, 1)
            halves[tile, rows, :] = jnp.where(lane < LANES // 2, packed[2 * tile], upper)
    for x in range(coarse.width):
        for no in range(5):
            for tile in range(coarse.tiles):
                coarse.sent[coarse_turn, 0, x + 1, pl.ds(no * coarse.tiles + tile, 1), :] = halves[
                    tile, pl.ds(5 * x + no, 1), :
                ]


def explode(coarse, coarse_turn, fine, fine_turn, pairs, halves):
    lane = lax.broadcasted_iota(jnp.int32, (ROWS, LANES), 1)
    for x in range(coarse.width):
        for no, q in enumerate(DOWNWARD):
            for tile in range(coarse.tiles):
                halves[tile, pl.ds(5 * x + no, 1), :] = coarse.relaxed[
                    coarse_turn, PLACE[q], x + 1, tile, pl.ds(0, 1), :
                ]
    for block in range((5 * coarse.width + ROWS - 1) // ROWS):
        rows = pl.ds(block * ROWS, ROWS)
        for tile in range(fine.tiles):
            value = halves[tile // 2, rows, :]
            if tile % 2 == 1:
                value = pltpu.roll(value, LANES // 2, 1)
            for bit in range(5, -1, -1):
                shifted = pltpu.roll(value, 2**bit, 1)
                value = jnp.where((lane & 2 ** (bit + 1)) != 0, shifted, value)
            value = jnp.where((lane & 1) != 0, pltpu.roll(value, 1, 1), value)
            pairs[tile, rows, :] = value
    for x in range(fine.width):
        for no in range(5):
            for tile in range(fine.tiles):
                fine.sent[fine_turn, 1, x + 1, pl.ds(no * fine.tiles + tile, 1), :] = pairs[
                    tile, pl.ds(5 * (x // 2) + no, 1), :
                ]


def kernel(
    sizes,
    coarse_in,
    medium_in,
    fine_in,
    solid_in,
    shear_ref,
    coarse_out,
    medium_out,
    fine_out,
    coarse_own,
    medium_own,
    fine_own,
    solid_own,
    pairs,
    halves,
    *rest,
):
    levels = []
    for t in range(3):
        levels.append(Level(2**t, 2**t, *rest[5 * t : 5 * t + 5]))
    coarse, medium, fine = levels
    own_sem, out_sem = rest[15:17]
    curve_size, level_size = sizes
    me_x, me_y = lax.axis_index("curve"), lax.axis_index("level")
    left, right = lax.rem(me_x + curve_size - 1, curve_size), lax.rem(me_x + 1, curve_size)
    below, above = lax.rem(me_y + level_size - 1, level_size), lax.rem(me_y + 1, level_size)
    around = ((left, right), (below, above), (me_x, me_y))
    at_bottom = me_y == 0
    at_top = me_y == level_size - 1

    def plane_load(x):
        return pltpu.make_async_copy(fine_in.at[:, pl.ds(x, 1)], fine_own.at[:, pl.ds(x, 1)], own_sem.at[x])

    def plane_store(x):
        return pltpu.make_async_copy(fine_own.at[:, pl.ds(x, 1)], fine_out.at[:, pl.ds(x, 1)], out_sem.at[x])

    solid_load = pltpu.make_async_copy(solid_in, solid_own, own_sem.at[4])
    medium_load = pltpu.make_async_copy(medium_in, medium_own, own_sem.at[5])
    coarse_load = pltpu.make_async_copy(coarse_in, coarse_own, own_sem.at[6])
    medium_store = pltpu.make_async_copy(medium_own, medium_out, out_sem.at[4])
    coarse_store = pltpu.make_async_copy(coarse_own, coarse_out, out_sem.at[5])
    solid_load.start()
    for x in range(4):
        plane_load(x).start()
    medium_load.start()
    coarse_load.start()

    barrier = pltpu.get_barrier_semaphore()
    for device in (
        (left, me_y),
        (right, me_y),
        (me_x, below),
        (me_x, above),
        (left, below),
        (left, above),
        (right, below),
        (right, above),
    ):
        pl.semaphore_signal(barrier, inc=1, device_id=device, device_id_type=pl.DeviceIdType.MESH)

    shear = jnp.broadcast_to(shear_ref[...], (ROWS, LANES))
    excess = 1.0 / shear - 0.5
    rates = [1.0 / (2.0**t * excess + 0.5) for t in range(3)]
    everywhere = list(range(1, 19))
    nowhere = []

    def solid_tile(x, tile):
        return solid_own[x, :, tile * LANES : (tile + 1) * LANES] == 1

    def taken(own, x, tile):
        return [own[q, x, :, tile * LANES : (tile + 1) * LANES] for q in range(19)]

    def sweep(level, body):
        def plane(x, carry):
            for tile in range(level.tiles):
                body(x, tile)
            return carry

        if level.width == 1:
            plane(0, 0)
        else:
            lax.fori_loop(0, level.width, plane, 0)

    def put(level, own, turn, blocked, solids):
        def body(x, tile):
            values = level.streamed(turn, x, tile, blocked)
            lanes = slice(tile * LANES, (tile + 1) * LANES)
            for q in range(19):
                value = values[q]
                if solids:
                    value = jnp.where(solid_tile(x, tile), own[q, x, :, lanes], value)
                own[q, x, :, lanes] = value

        return body

    def send(level, turn):
        for copy in level.copies(turn, around):
            copy.start()

    def receive(level, turn):
        for copy in level.copies(turn, around):
            copy.wait_recv()

    def no_wall_above(turn):
        fine.sent[turn, 0] = jnp.full(fine.sent.shape[2:], SOLID, jnp.float32)

    solid_load.wait()

    def first_plane(x, carry):
        plane_load(x).wait()
        for tile in range(fine.tiles):
            fine.keep(0, x, tile, collide(taken(fine_own, x, tile), rates[2], solid_tile(x, tile)))
        return carry

    lax.fori_loop(0, fine.width, first_plane, 0)
    medium_load.wait()
    sweep(medium, lambda x, tile: medium.keep(0, x, tile, collide(taken(medium_own, x, tile), rates[1], None)))
    coarse_load.wait()
    sweep(coarse, lambda x, tile: coarse.keep(0, x, tile, collide(taken(coarse_own, x, tile), rates[0], None)))

    @pl.when(at_top)
    def _():
        no_wall_above(0)
        coalesce(fine, 0, medium, 0, pairs, halves)
        coalesce(medium, 0, coarse, 0, pairs, halves)

    @pl.when(at_bottom)
    def _():
        coarse.sent[0, 1] = jnp.full(coarse.sent.shape[2:], SOLID, jnp.float32)
        explode(medium, 0, fine, 0, pairs, halves)
        explode(coarse, 0, medium, 0, pairs, halves)

    pl.semaphore_wait(barrier, 8)
    send(fine, 0)
    send(medium, 0)
    send(coarse, 0)
    receive(fine, 0)

    def again(turn):
        def body(x, tile):
            values = fine.streamed(turn - 1, x, tile, everywhere)
            fine.keep(turn, x, tile, collide(values, rates[2], solid_tile(x, tile)))

        return body

    sweep(fine, again(1))

    @pl.when(at_top)
    def _():
        no_wall_above(1)

    @pl.when(at_bottom)
    def _():
        fine.sent[1, 1] = fine.sent[0, 1]

    send(fine, 1)
    receive(medium, 0)
    sweep(
        medium,
        lambda x, tile: medium.keep(1, x, tile, collide(medium.streamed(0, x, tile, nowhere), rates[1], None)),
    )
    receive(coarse, 0)
    sweep(coarse, put(coarse, coarse_own, 0, DOWNWARD, False))
    coarse_store.start()

    receive(fine, 1)
    sweep(fine, again(2))

    @pl.when(at_top)
    def _():
        no_wall_above(2)
        coalesce(fine, 2, medium, 1, pairs, halves)

    @pl.when(at_bottom)
    def _():
        explode(medium, 1, fine, 2, pairs, halves)
        medium.sent[1, 1] = medium.sent[0, 1]

    send(fine, 2)
    send(medium, 1)
    receive(fine, 2)

    sweep(fine, again(3))

    @pl.when(at_top)
    def _():
        no_wall_above(3)

    @pl.when(at_bottom)
    def _():
        fine.sent[3, 1] = fine.sent[2, 1]

    send(fine, 3)
    receive(medium, 1)
    sweep(medium, put(medium, medium_own, 1, nowhere, False))
    medium_store.start()
    receive(fine, 3)
    last = put(fine, fine_own, 3, everywhere, True)

    def last_plane(x, carry):
        for tile in range(fine.tiles):
            last(x, tile)
        plane_store(x).start()
        return carry

    lax.fori_loop(0, fine.width, last_plane, 0)
    for level, turns in ((fine, 4), (medium, 2), (coarse, 1)):
        for turn in range(turns):
            for copy in level.copies(turn, around):
                copy.wait_send()
    coarse_store.wait()
    medium_store.wait()
    for x in range(4):
        plane_store(x).wait()


def shards(coarse_pops, medium_pops, fine_pops, solid_cells, shear_rate):
    sizes = (lax.axis_size("curve"), lax.axis_size("level"))
    scratch = [
        pltpu.VMEM(coarse_pops.shape, jnp.float32),
        pltpu.VMEM(medium_pops.shape, jnp.float32),
        pltpu.VMEM(fine_pops.shape, jnp.float32),
        pltpu.VMEM(solid_cells.shape, jnp.int32),
        pltpu.VMEM((4, 16, LANES), jnp.float32),
        pltpu.VMEM((2, 16, LANES), jnp.float32),
    ]
    for t, turns in ((0, 1), (1, 2), (2, 4)):
        width = tiles = 2**t
        lines = (5 * tiles + ROWS - 1) // ROWS * ROWS
        scratch += [
            pltpu.VMEM((turns, 19, width + 2, tiles, ROWS, LANES), jnp.float32),
            pltpu.VMEM((turns, 2, width + 2, lines, LANES), jnp.float32),
            pltpu.VMEM((turns, 2, width + 2, lines, LANES), jnp.float32),
            pltpu.SemaphoreType.DMA((turns, 8)),
            pltpu.SemaphoreType.DMA((turns, 8)),
        ]
    scratch += [pltpu.SemaphoreType.DMA((7,)), pltpu.SemaphoreType.DMA((6,))]
    whole = pl.BlockSpec(memory_space=pl.ANY)
    return pl.pallas_call(
        lambda *refs: kernel(sizes, *refs),
        out_shape=tuple(
            jax.ShapeDtypeStruct(pops.shape, jnp.float32) for pops in (coarse_pops, medium_pops, fine_pops)
        ),
        in_specs=[whole] * 4 + [pl.BlockSpec(memory_space=pltpu.VMEM)],
        out_specs=(whole,) * 3,
        scratch_shapes=scratch,
        compiler_params=pltpu.CompilerParams(
            collective_id=0, has_side_effects=True, vmem_limit_bytes=48 * 1024 * 1024
        ),
    )(coarse_pops, medium_pops, fine_pops, solid_cells, shear_rate)


def solution(mesh):
    lattice = P(None, "curve", "level", None)
    return jax.shard_map(
        shards,
        mesh=mesh,
        in_specs=(lattice, lattice, lattice, P("curve", "level", None), P("curve", "level")),
        out_specs=(lattice, lattice, lattice),
        check_vma=False,
    )
```

```python
import jax
import jax.numpy as jnp
from jax import lax
from jax.experimental import pallas as pl
from jax.experimental.pallas import tpu as pltpu
from jax.sharding import PartitionSpec as P

VELOCITIES = [
    (0, 0, 0),
    (1, 0, 0),
    (-1, 0, 0),
    (0, 1, 0),
    (0, -1, 0),
    (0, 0, 1),
    (0, 0, -1),
    (1, 1, 0),
    (-1, -1, 0),
    (1, -1, 0),
    (-1, 1, 0),
    (1, 0, 1),
    (-1, 0, -1),
    (1, 0, -1),
    (-1, 0, 1),
    (0, 1, 1),
    (0, -1, -1),
    (0, 1, -1),
    (0, -1, 1),
]
OPPOSITE = [0, 2, 1, 4, 3, 6, 5, 8, 7, 10, 9, 12, 11, 14, 13, 16, 15, 18, 17]

ORDER = [1, 7, 9, 11, 13, 2, 8, 10, 12, 14, 0, 3, 4, 5, 6, 15, 16, 17, 18]
PLACE = [ORDER.index(q) for q in range(19)]
UPWARD = [7, 3, 10, 15, 17]
DOWNWARD = [9, 4, 8, 16, 18]
ROWS = 8
LANES = 128
SUBSTEPS = 4
EVERY = tuple(range(1, 19))
CORNERS_FIRST = (4, 5, 6, 7, 0, 1, 2, 3)
SOLID = float("nan")


def collide(f, rate, solid):
    s = {}
    d = {}
    for q in (1, 3, 5, 7, 9, 11, 13, 15, 17):
        s[q] = f[q] + f[q + 1]
        d[q] = f[q] - f[q + 1]
    xy, xz, yz = s[7] + s[9], s[11] + s[13], s[15] + s[17]
    pxy, pxz, pyz = s[7] - s[9], s[11] - s[13], s[15] - s[17]
    axis_sum = s[1] + s[3] + s[5]
    edge_sum = xy + xz + yz
    density = f[0] + axis_sum + edge_sum
    if solid is not None:
        density = jnp.where(solid, SOLID, density)
    inverse = 1.0 / density
    x_xy, y_xy = d[7] + d[9], d[7] - d[9]
    x_xz, z_xz = d[11] + d[13], d[11] - d[13]
    y_yz, z_yz = d[15] + d[17], d[15] - d[17]
    sum_x, sum_y, sum_z = x_xy + x_xz, y_xy + y_yz, z_xz + z_yz
    jx, jy, jz = d[1] + sum_x, d[3] + sum_y, d[5] + sum_z
    ux, uy, uz = jx * inverse, jy * inverse, jz * inverse
    xx, yy, zz = jx * ux, jy * uy, jz * uz
    yy_zz = yy + zz
    energy = xx + yy_zz

    tx, ty, tz = sum_x - 2.0 * d[1], sum_y - 2.0 * d[3], sum_z - 2.0 * d[5]
    mx = 0.2475 * (x_xy - x_xz)
    my = 0.2475 * (y_yz - y_xy)
    mz = 0.2475 * (z_xz - z_yz)
    hx, hy, hz = 0.05 * tx, 0.05 * ty, 0.05 * tz
    ax, ay, az = 0.2 * tx, 0.2 * ty, 0.2 * tz
    x1, x2 = hx + mx, hx - mx
    y1, y2 = hy - my, hy + my
    z1, z2 = hz + mz, hz - mz

    alpha = (1.19 * 19.0 / 2394.0) * (edge_sum - f[0] - energy)
    beta = (1.4 / 252.0) * (9.0 * f[0] - 7.0 * axis_sum - 2.0 * edge_sum + 5.5 * energy)
    base0 = 30.0 * alpha - 12.0 * beta
    base1 = 11.0 * alpha + 4.0 * beta
    base2 = 8.0 * alpha + beta
    u1 = 3.0 * s[1] - axis_sum
    u2 = edge_sum - 3.0 * yz
    pxx = 2.0 * xx - yy_zz
    gamma = (rate * (1.0 / 36.0)) * (u1 + u2 - pxx)
    delta = (1.4 / 72.0) * (u2 - 2.0 * u1 + 0.5 * pxx)
    v1 = s[3] - s[5]
    v2 = xy - xz
    ww = yy - zz
    eps = (rate * (1.0 / 12.0)) * (v1 + v2 - ww)
    zeta = (1.4 / 24.0) * (v2 - 2.0 * v1 + 0.5 * ww)
    g1, g2 = gamma - 2.0 * delta, gamma + delta
    h1, h2 = eps - 2.0 * zeta, eps + zeta
    quarter = rate * 0.25
    nxy = quarter * (pxy - jx * uy)
    nxz = quarter * (pxz - jx * uz)
    nyz = quarter * (pyz - jy * uz)
    ex = base1 - 2.0 * g1
    eyz = base1 + g1
    ey, ez = eyz - h1, eyz + h1
    low = base2 + g2
    exy, exz = low + h2, low - h2
    eyz2 = base2 - 2.0 * g2
    out = [None] * 19
    out[0] = f[0] + base0
    for q, even, odd in ((1, ex, ax), (3, ey, ay), (5, ez, az)):
        out[q] = f[q] + (even + odd)
        out[q + 1] = f[q + 1] + (even - odd)
    for q, even, odd in (
        (7, exy + nxy, x1 + y1),
        (9, exy - nxy, x1 - y1),
        (11, exz + nxz, x2 + z1),
        (13, exz - nxz, x2 - z1),
        (15, eyz2 + nyz, y2 + z2),
        (17, eyz2 - nyz, y2 - z2),
    ):
        out[q] = f[q] - (even + odd)
        out[q + 1] = f[q + 1] - (even - odd)
    return out


class Level:
    def __init__(self, width, tiles, relaxed, sent, came, send_sem, recv_sem):
        self.width, self.tiles = width, tiles
        self.relaxed, self.sent, self.came = relaxed, sent, came
        self.send_sem, self.recv_sem = send_sem, recv_sem

    def copies(self, turn, around):
        width, tiles = self.width, self.tiles
        third = (2 * tiles // ROWS) * ROWS
        relaxed, sent, came = self.relaxed, self.sent, self.came
        (left, right), (below, above), (me_x, me_y) = around

        def copy(no, source, target, device):
            return lambda: pltpu.make_async_remote_copy(
                src_ref=source,
                dst_ref=target,
                send_sem=self.send_sem.at[turn, no],
                recv_sem=self.recv_sem.at[turn, no],
                device_id=device,
                device_id_type=pl.DeviceIdType.MESH,
            )

        rows = pl.ds(1, width)
        first, last = pl.ds(0, ROWS), pl.ds(third, ROWS)
        result = [
            copy(0, relaxed.at[turn, pl.ds(0, 5), width], relaxed.at[turn, pl.ds(0, 5), 0], (right, me_y)),
            copy(1, relaxed.at[turn, pl.ds(5, 5), 1], relaxed.at[turn, pl.ds(5, 5), width + 1], (left, me_y)),
        ]
        for way, beyond in ((0, above), (1, below)):
            result.append(copy(2 + way, sent.at[turn, way, rows], came.at[turn, way, rows], (me_x, beyond)))
        for way, beyond in ((0, above), (1, below)):
            result.append(
                copy(4 + way, sent.at[turn, way, width, first], came.at[turn, way, 0, first], (right, beyond))
            )
            result.append(
                copy(6 + way, sent.at[turn, way, 1, last], came.at[turn, way, width + 1, last], (left, beyond))
            )
        return result

    def keep(self, turn, x, tile, values):
        for q in range(19):
            self.relaxed[turn, PLACE[q], x + 1, tile] = values[q]
        for way, group, row in ((0, UPWARD, ROWS - 1), (1, DOWNWARD, 0)):
            for no, q in enumerate(group):
                self.sent[turn, way, x + 1, pl.ds(no * self.tiles + tile, 1), :] = values[q][row : row + 1, :]

    def streamed(self, turn, x, tile, blocked):
        lane = lax.broadcasted_iota(jnp.int32, (ROWS, LANES), 1)
        row = lax.broadcasted_iota(jnp.int32, (ROWS, LANES), 0)
        relaxed, came, tiles = self.relaxed, self.came, self.tiles
        values = []
        for q, (step_x, step_y, step_z) in enumerate(VELOCITIES):
            plane = x + 1 - step_x
            place = PLACE[q]
            value = relaxed[turn, place, plane, tile]
            beside = (tile - step_z) % tiles
            crossing = lane == (LANES - 1 if step_z > 0 else 0)
            if step_z != 0 and tiles > 1:
                value = jnp.where(crossing, relaxed[turn, place, plane, beside], value)
            if step_y != 0:
                way = 0 if step_y > 0 else 1
                no = (UPWARD if step_y > 0 else DOWNWARD).index(q) * tiles

                def ghost(at):
                    line = came[turn, way, plane, pl.ds(no + at, 1), :]
                    return jnp.broadcast_to(line, (ROWS, LANES))

                edge = ghost(tile)
                if step_z != 0 and tiles > 1:
                    edge = jnp.where(crossing, ghost(beside), edge)
                value = pltpu.roll(value, 1 if step_y > 0 else ROWS - 1, 0)
                value = jnp.where(row == (0 if step_y > 0 else ROWS - 1), edge, value)
            if step_z != 0:
                value = pltpu.roll(value, 1 if step_z > 0 else LANES - 1, 1)
            if q in blocked:
                value = jnp.where(value != value, relaxed[turn, PLACE[OPPOSITE[q]], x + 1, tile], value)
            values.append(value)
        return values


def solid_tile(solid, x, tile):
    return solid[x, :, tile * LANES : (tile + 1) * LANES] == 1


def coalesce(fine, fine_turn, coarse, coarse_turn, pairs, halves):
    lane = lax.broadcasted_iota(jnp.int32, (ROWS, LANES), 1)
    for x in range(coarse.width):
        for no, q in enumerate(UPWARD):
            for tile in range(fine.tiles):
                both = (
                    fine.relaxed[fine_turn, PLACE[q], 2 * x + 1, tile]
                    + fine.relaxed[fine_turn, PLACE[q], 2 * x + 2, tile]
                )
                both = both + pltpu.roll(both, 1, 0)
                pairs[tile, pl.ds(5 * x + no, 1), :] = both[ROWS - 1 : ROWS, :]
    for block in range((5 * coarse.width + ROWS - 1) // ROWS):
        rows = pl.ds(block * ROWS, ROWS)
        packed = []
        for tile in range(fine.tiles):
            value = pairs[tile, rows, :]
            value = (value + pltpu.roll(value, LANES - 1, 1)) * 0.125
            for bit in range(6):
                shifted = pltpu.roll(value, LANES - 2**bit, 1)
                value = jnp.where((lane & 2**bit) != 0, shifted, value)
            packed.append(value)
        for tile in range(coarse.tiles):
            upper = pltpu.roll(packed[2 * tile + 1], LANES // 2, 1)
            halves[tile, rows, :] = jnp.where(lane < LANES // 2, packed[2 * tile], upper)
    for x in range(coarse.width):
        for no in range(5):
            for tile in range(coarse.tiles):
                coarse.sent[coarse_turn, 0, x + 1, pl.ds(no * coarse.tiles + tile, 1), :] = halves[
                    tile, pl.ds(5 * x + no, 1), :
                ]


def explode(coarse, coarse_turn, target, fine, pairs, halves):
    lane = lax.broadcasted_iota(jnp.int32, (ROWS, LANES), 1)
    for x in range(coarse.width):
        for no, q in enumerate(DOWNWARD):
            for tile in range(coarse.tiles):
                halves[tile, pl.ds(5 * x + no, 1), :] = coarse.relaxed[
                    coarse_turn, PLACE[q], x + 1, tile, pl.ds(0, 1), :
                ]
    for block in range((5 * coarse.width + ROWS - 1) // ROWS):
        rows = pl.ds(block * ROWS, ROWS)
        for tile in range(fine.tiles):
            value = halves[tile // 2, rows, :]
            if tile % 2 == 1:
                value = pltpu.roll(value, LANES // 2, 1)
            for bit in range(5, -1, -1):
                shifted = pltpu.roll(value, 2**bit, 1)
                value = jnp.where((lane & 2 ** (bit + 1)) != 0, shifted, value)
            value = jnp.where((lane & 1) != 0, pltpu.roll(value, 1, 1), value)
            pairs[tile, rows, :] = value
    for x in range(fine.width):
        for no in range(5):
            for tile in range(fine.tiles):
                target[x + 1, pl.ds(no * fine.tiles + tile, 1), :] = pairs[
                    tile, pl.ds(5 * (x // 2) + no, 1), :
                ]


def kernel(
    sizes,
    coarse_in,
    medium_in,
    fine_in,
    solid_in,
    shear_ref,
    coarse_own,
    medium_own,
    fine_own,
    solid_own,
    fine_relaxed,
    fine_came,
    pairs,
    halves,
    exploded,
    own_sem,
    *rest,
):
    coarse = Level(1, 1, *rest[:5])
    medium = Level(2, 2, *rest[5:10])
    fine = Level(4, 4, fine_relaxed, rest[10], fine_came, *rest[11:])
    curve_size, level_size = sizes
    me_x, me_y = lax.axis_index("curve"), lax.axis_index("level")
    left, right = lax.rem(me_x + curve_size - 1, curve_size), lax.rem(me_x + 1, curve_size)
    below, above = lax.rem(me_y + level_size - 1, level_size), lax.rem(me_y + 1, level_size)
    around = ((left, right), (below, above), (me_x, me_y))
    at_bottom = me_y == 0
    at_top = me_y == level_size - 1

    def plane_load(x):
        return pltpu.make_async_copy(fine_in.at[:, pl.ds(x, 1)], fine_own.at[:, pl.ds(x, 1)], own_sem.at[x])

    solid_load = pltpu.make_async_copy(solid_in, solid_own, own_sem.at[4])
    medium_load = pltpu.make_async_copy(medium_in, medium_own, own_sem.at[5])
    coarse_load = pltpu.make_async_copy(coarse_in, coarse_own, own_sem.at[6])
    medium_load.start()
    for x in (0, 3):
        plane_load(x).start()
    solid_load.start()
    for x in (1, 2):
        plane_load(x).start()
    coarse_load.start()

    barrier = pltpu.get_barrier_semaphore()
    for device in (
        (left, me_y),
        (right, me_y),
        (me_x, below),
        (me_x, above),
        (left, below),
        (left, above),
        (right, below),
        (right, above),
    ):
        pl.semaphore_signal(barrier, inc=1, device_id=device, device_id_type=pl.DeviceIdType.MESH)

    shear = jnp.broadcast_to(shear_ref[...], (ROWS, LANES))
    excess = 1.0 / shear - 0.5
    rates = [1.0 / (2.0**t * excess + 0.5) for t in range(3)]

    def taken(own, x, tile):
        return [own[q, x, :, tile * LANES : (tile + 1) * LANES] for q in range(19)]

    def sweep(level, body):
        def plane(x, carry):
            for tile in range(level.tiles):
                body(x, tile)
            return carry

        if level.width == 1:
            plane(0, 0)
        else:
            lax.fori_loop(0, level.width, plane, 0)

    def put(level, own, turn, blocked):
        def body(x, tile):
            values = level.streamed(turn, x, tile, blocked)
            for q in range(19):
                own[q, x, :, tile * LANES : (tile + 1) * LANES] = values[q]

        return body

    def send(level, turn, which):
        copies = level.copies(turn, around)
        for no in which:
            copies[no]().start()

    def receive(level, turn):
        for copy in level.copies(turn, around):
            copy().wait_recv()

    def sent_off(level, turn):
        for copy in level.copies(turn, around):
            copy().wait_send()

    def wall_above(turn, x):
        fine.sent[turn, 0, x + 1] = jnp.full(fine.sent.shape[3:], SOLID, jnp.float32)

    def edges(turn, x):
        @pl.when(at_top)
        def _():
            wall_above(turn, x)

        @pl.when(at_bottom)
        def _():
            fine.sent[turn, 1, x + 1] = exploded[x + 1]

    def fine_pass(turn, relax):
        def plane(step, carry):
            x = jnp.where(step < 2, 3 * step, step - 1)
            relax(x)
            edges(turn, x)

            @pl.when(step == 1)
            def _():
                send(fine, turn, (4, 5, 6, 7, 0, 1))

            return carry

        lax.fori_loop(0, fine.width, plane, 0)
        send(fine, turn, (2, 3))

    medium_load.wait()
    sweep(medium, lambda x, tile: medium.keep(0, x, tile, collide(taken(medium_own, x, tile), rates[1], None)))

    @pl.when(at_bottom)
    def _():
        explode(medium, 0, exploded, fine, pairs, halves)

    solid_load.wait()
    pl.semaphore_wait(barrier, 8)

    def first(x):
        plane_load(x).wait()
        for tile in range(fine.tiles):
            fine.keep(0, x, tile, collide(taken(fine_own, x, tile), rates[2], solid_tile(solid_own, x, tile)))

    fine_pass(0, first)
    coarse_load.wait()
    sweep(coarse, lambda x, tile: coarse.keep(0, x, tile, collide(taken(coarse_own, x, tile), rates[0], None)))

    @pl.when(at_top)
    def _():
        coalesce(fine, 0, medium, 0, pairs, halves)
        coalesce(medium, 0, coarse, 0, pairs, halves)

    @pl.when(at_bottom)
    def _():
        coarse.sent[0, 1] = jnp.full(coarse.sent.shape[2:], SOLID, jnp.float32)
        explode(coarse, 0, medium.sent.at[0, 1], medium, pairs, halves)

    send(medium, 0, CORNERS_FIRST)
    send(coarse, 0, CORNERS_FIRST)

    def substep(turn, carry):
        receive(fine, turn - 1)

        def again(x):
            for tile in range(fine.tiles):
                values = fine.streamed(turn - 1, x, tile, EVERY)
                fine.keep(turn, x, tile, collide(values, rates[2], solid_tile(solid_own, x, tile)))

        fine_pass(turn, again)

        @pl.when(turn == 1)
        def _():
            receive(medium, 0)
            sweep(
                medium,
                lambda x, tile: medium.keep(1, x, tile, collide(medium.streamed(0, x, tile, ()), rates[1], None)),
            )

            @pl.when(at_bottom)
            def _():
                explode(medium, 1, exploded, fine, pairs, halves)
                medium.sent[1, 1] = medium.sent[0, 1]

            receive(coarse, 0)
            sweep(coarse, put(coarse, coarse_own, 0, DOWNWARD))

        @pl.when(turn == 2)
        def _():
            @pl.when(at_top)
            def _():
                coalesce(fine, 2, medium, 1, pairs, halves)

            send(medium, 1, CORNERS_FIRST)

        return carry

    lax.fori_loop(1, SUBSTEPS, substep, 0)
    receive(medium, 1)
    sweep(medium, put(medium, medium_own, 1, ()))
    sent_off(coarse, 0)
    sent_off(medium, 0)
    sent_off(medium, 1)
    for turn in range(SUBSTEPS - 1):
        sent_off(fine, turn)
    receive(fine, SUBSTEPS - 1)
    sent_off(fine, SUBSTEPS - 1)


def finish(coarse, medium, fine_pops, solid, fine_relaxed, fine_came, coarse_out, medium_out, fine_out, own, sem):
    others = [
        pltpu.make_async_copy(source, target, sem.at[no])
        for no, (source, target) in enumerate(((medium, medium_out), (coarse, coarse_out)))
    ]
    for copy in others:
        copy.start()

    def plane_store(x):
        return pltpu.make_async_copy(own.at[:, pl.ds(x, 1)], fine_out.at[:, pl.ds(x, 1)], sem.at[2 + x])

    fine = Level(4, 4, fine_relaxed, None, fine_came, None, None)

    def plane(x, carry):
        for tile in range(fine.tiles):
            values = fine.streamed(SUBSTEPS - 1, x, tile, EVERY)
            lanes = slice(tile * LANES, (tile + 1) * LANES)
            for q in range(19):
                own[q, x, :, lanes] = jnp.where(solid_tile(solid, x, tile), fine_pops[q, x, :, lanes], values[q])
        plane_store(x).start()
        return carry

    lax.fori_loop(0, fine.width, plane, 0)
    for copy in others:
        copy.wait()
    for x in range(fine.width):
        plane_store(x).wait()


def shards(coarse_pops, medium_pops, fine_pops, solid_cells, shear_rate):
    sizes = (lax.axis_size("curve"), lax.axis_size("level"))
    scratch = [
        pltpu.VMEM((4, 16, LANES), jnp.float32),
        pltpu.VMEM((2, 16, LANES), jnp.float32),
        pltpu.VMEM((6, 24, LANES), jnp.float32),
        pltpu.SemaphoreType.DMA((7,)),
    ]
    for t, turns in ((0, 1), (1, 2), (2, SUBSTEPS)):
        width = tiles = 2**t
        lines = (5 * tiles + ROWS - 1) // ROWS * ROWS
        relaxed = pltpu.VMEM((turns, 19, width + 2, tiles, ROWS, LANES), jnp.float32)
        edge_rows = pltpu.VMEM((turns, 2, width + 2, lines, LANES), jnp.float32)
        scratch += [edge_rows] if t == 2 else [relaxed, edge_rows, edge_rows]
        scratch += [pltpu.SemaphoreType.DMA((turns, 8))] * 2
    given = (coarse_pops, medium_pops, fine_pops, solid_cells)
    in_vmem = pl.BlockSpec(memory_space=pltpu.VMEM)
    held = pl.pallas_call(
        lambda *refs: kernel(sizes, *refs),
        out_shape=tuple(pltpu.VMEM(array.shape, array.dtype) for array in given) + (relaxed, edge_rows),
        in_specs=[pl.BlockSpec(memory_space=pltpu.HBM)] * 4 + [in_vmem],
        out_specs=(in_vmem,) * 6,
        scratch_shapes=scratch,
        compiler_params=pltpu.CompilerParams(
            collective_id=0, has_side_effects=True, vmem_limit_bytes=24 * 1024 * 1024
        ),
    )(*[pltpu.with_memory_space_constraint(array, pltpu.HBM) for array in given], shear_rate)
    return pl.pallas_call(
        finish,
        out_shape=tuple(jax.ShapeDtypeStruct(pops.shape, jnp.float32) for pops in given[:3]),
        in_specs=[in_vmem] * 6,
        out_specs=(pl.BlockSpec(memory_space=pl.ANY),) * 3,
        scratch_shapes=[pltpu.VMEM(fine_pops.shape, jnp.float32), pltpu.SemaphoreType.DMA((6,))],
        compiler_params=pltpu.CompilerParams(vmem_limit_bytes=24 * 1024 * 1024),
    )(*held)


def solution(mesh):
    lattice = P(None, "curve", "level", None)
    return jax.shard_map(
        shards,
        mesh=mesh,
        in_specs=(lattice, lattice, lattice, P("curve", "level", None), P("curve", "level")),
        out_specs=(lattice, lattice, lattice),
        check_vma=False,
    )
```

```python
import jax
import jax.numpy as jnp
from jax import lax
from jax.experimental import pallas as pl
from jax.experimental.pallas import tpu as pltpu
from jax.sharding import PartitionSpec as P

VELOCITIES = [
    (0, 0, 0),
    (1, 0, 0),
    (-1, 0, 0),
    (0, 1, 0),
    (0, -1, 0),
    (0, 0, 1),
    (0, 0, -1),
    (1, 1, 0),
    (-1, -1, 0),
    (1, -1, 0),
    (-1, 1, 0),
    (1, 0, 1),
    (-1, 0, -1),
    (1, 0, -1),
    (-1, 0, 1),
    (0, 1, 1),
    (0, -1, -1),
    (0, 1, -1),
    (0, -1, 1),
]
OPPOSITE = [0, 2, 1, 4, 3, 6, 5, 8, 7, 10, 9, 12, 11, 14, 13, 16, 15, 18, 17]

ORDER = [1, 7, 9, 11, 13, 2, 8, 10, 12, 14, 0, 3, 4, 5, 6, 15, 16, 17, 18]
PLACE = [ORDER.index(q) for q in range(19)]
UPWARD = [7, 3, 10, 15, 17]
DOWNWARD = [9, 4, 8, 16, 18]
ROWS = 8
LANES = 128
SUBSTEPS = 4
EVERY = tuple(range(1, 19))
FROM_LEFT = (4, 5, 0)
FROM_RIGHT = (6, 7, 1)
ROWS_ONLY = (2, 3)
CORNERS_FIRST = (4, 5, 6, 7, 0, 1, 2, 3)
SOLID = float("nan")


def collide(f, rate, solid):
    s = {}
    d = {}
    for q in (1, 3, 5, 7, 9, 11, 13, 15, 17):
        s[q] = f[q] + f[q + 1]
        d[q] = f[q] - f[q + 1]
    xy, xz, yz = s[7] + s[9], s[11] + s[13], s[15] + s[17]
    pxy, pxz, pyz = s[7] - s[9], s[11] - s[13], s[15] - s[17]
    axis_sum = s[1] + s[3] + s[5]
    edge_sum = xy + xz + yz
    density = f[0] + axis_sum + edge_sum
    if solid is not None:
        density = jnp.where(solid, SOLID, density)
    inverse = 1.0 / density
    x_xy, y_xy = d[7] + d[9], d[7] - d[9]
    x_xz, z_xz = d[11] + d[13], d[11] - d[13]
    y_yz, z_yz = d[15] + d[17], d[15] - d[17]
    sum_x, sum_y, sum_z = x_xy + x_xz, y_xy + y_yz, z_xz + z_yz
    jx, jy, jz = d[1] + sum_x, d[3] + sum_y, d[5] + sum_z
    ux, uy, uz = jx * inverse, jy * inverse, jz * inverse
    xx, yy, zz = jx * ux, jy * uy, jz * uz
    yy_zz = yy + zz
    energy = xx + yy_zz

    tx, ty, tz = sum_x - 2.0 * d[1], sum_y - 2.0 * d[3], sum_z - 2.0 * d[5]
    mx = 0.2475 * (x_xy - x_xz)
    my = 0.2475 * (y_yz - y_xy)
    mz = 0.2475 * (z_xz - z_yz)
    hx, hy, hz = 0.05 * tx, 0.05 * ty, 0.05 * tz
    ax, ay, az = 0.2 * tx, 0.2 * ty, 0.2 * tz
    x1, x2 = hx + mx, hx - mx
    y1, y2 = hy - my, hy + my
    z1, z2 = hz + mz, hz - mz

    alpha = (1.19 * 19.0 / 2394.0) * (edge_sum - f[0] - energy)
    beta = (1.4 / 252.0) * (9.0 * f[0] - 7.0 * axis_sum - 2.0 * edge_sum + 5.5 * energy)
    base0 = 30.0 * alpha - 12.0 * beta
    base1 = 11.0 * alpha + 4.0 * beta
    base2 = 8.0 * alpha + beta
    u1 = 3.0 * s[1] - axis_sum
    u2 = edge_sum - 3.0 * yz
    pxx = 2.0 * xx - yy_zz
    gamma = (rate * (1.0 / 36.0)) * (u1 + u2 - pxx)
    delta = (1.4 / 72.0) * (u2 - 2.0 * u1 + 0.5 * pxx)
    v1 = s[3] - s[5]
    v2 = xy - xz
    ww = yy - zz
    eps = (rate * (1.0 / 12.0)) * (v1 + v2 - ww)
    zeta = (1.4 / 24.0) * (v2 - 2.0 * v1 + 0.5 * ww)
    g1, g2 = gamma - 2.0 * delta, gamma + delta
    h1, h2 = eps - 2.0 * zeta, eps + zeta
    quarter = rate * 0.25
    nxy = quarter * (pxy - jx * uy)
    nxz = quarter * (pxz - jx * uz)
    nyz = quarter * (pyz - jy * uz)
    ex = base1 - 2.0 * g1
    eyz = base1 + g1
    ey, ez = eyz - h1, eyz + h1
    low = base2 + g2
    exy, exz = low + h2, low - h2
    eyz2 = base2 - 2.0 * g2
    out = [None] * 19
    out[0] = f[0] + base0
    for q, even, odd in ((1, ex, ax), (3, ey, ay), (5, ez, az)):
        out[q] = f[q] + (even + odd)
        out[q + 1] = f[q + 1] + (even - odd)
    for q, even, odd in (
        (7, exy + nxy, x1 + y1),
        (9, exy - nxy, x1 - y1),
        (11, exz + nxz, x2 + z1),
        (13, exz - nxz, x2 - z1),
        (15, eyz2 + nyz, y2 + z2),
        (17, eyz2 - nyz, y2 - z2),
    ):
        out[q] = f[q] - (even + odd)
        out[q + 1] = f[q + 1] - (even - odd)
    return out


class Level:
    def __init__(self, width, tiles, relaxed, sent, came, send_sem, recv_sem):
        self.width, self.tiles = width, tiles
        self.relaxed, self.sent, self.came = relaxed, sent, came
        self.send_sem, self.recv_sem = send_sem, recv_sem

    def copies(self, turn, around):
        width, tiles = self.width, self.tiles
        third = (2 * tiles // ROWS) * ROWS
        relaxed, sent, came = self.relaxed, self.sent, self.came
        (left, right), (below, above), (me_x, me_y) = around

        def copy(no, source, target, device):
            return lambda: pltpu.make_async_remote_copy(
                src_ref=source,
                dst_ref=target,
                send_sem=self.send_sem.at[turn, no],
                recv_sem=self.recv_sem.at[turn, no],
                device_id=device,
                device_id_type=pl.DeviceIdType.MESH,
            )

        rows = pl.ds(1, width)
        first, last = pl.ds(0, ROWS), pl.ds(third, ROWS)
        result = [
            copy(0, relaxed.at[turn, pl.ds(0, 5), width], relaxed.at[turn, pl.ds(0, 5), 0], (right, me_y)),
            copy(1, relaxed.at[turn, pl.ds(5, 5), 1], relaxed.at[turn, pl.ds(5, 5), width + 1], (left, me_y)),
        ]
        for way, beyond in ((0, above), (1, below)):
            result.append(copy(2 + way, sent.at[turn, way, rows], came.at[turn, way, rows], (me_x, beyond)))
        for way, beyond in ((0, above), (1, below)):
            result.append(
                copy(4 + way, sent.at[turn, way, width, first], came.at[turn, way, 0, first], (right, beyond))
            )
        for way, beyond in ((0, above), (1, below)):
            result.append(
                copy(6 + way, sent.at[turn, way, 1, last], came.at[turn, way, width + 1, last], (left, beyond))
            )
        return result

    def keep(self, turn, x, tile, values):
        for q in range(19):
            self.relaxed[turn, PLACE[q], x + 1, tile] = values[q]
        for way, group, row in ((0, UPWARD, ROWS - 1), (1, DOWNWARD, 0)):
            for no, q in enumerate(group):
                self.sent[turn, way, x + 1, pl.ds(no * self.tiles + tile, 1), :] = values[q][row : row + 1, :]

    def streamed(self, turn, x, tile, blocked):
        lane = lax.broadcasted_iota(jnp.int32, (ROWS, LANES), 1)
        row = lax.broadcasted_iota(jnp.int32, (ROWS, LANES), 0)
        relaxed, came, tiles = self.relaxed, self.came, self.tiles
        values = []
        for q, (step_x, step_y, step_z) in enumerate(VELOCITIES):
            plane = x + 1 - step_x
            place = PLACE[q]
            value = relaxed[turn, place, plane, tile]
            beside = (tile - step_z) % tiles
            crossing = lane == (LANES - 1 if step_z > 0 else 0)
            if step_z != 0 and tiles > 1:
                value = jnp.where(crossing, relaxed[turn, place, plane, beside], value)
            if step_y != 0:
                way = 0 if step_y > 0 else 1
                no = (UPWARD if step_y > 0 else DOWNWARD).index(q) * tiles

                def ghost(at):
                    line = came[turn, way, plane, pl.ds(no + at, 1), :]
                    return jnp.broadcast_to(line, (ROWS, LANES))

                edge = ghost(tile)
                if step_z != 0 and tiles > 1:
                    edge = jnp.where(crossing, ghost(beside), edge)
                value = pltpu.roll(value, 1 if step_y > 0 else ROWS - 1, 0)
                value = jnp.where(row == (0 if step_y > 0 else ROWS - 1), edge, value)
            if step_z != 0:
                value = pltpu.roll(value, 1 if step_z > 0 else LANES - 1, 1)
            if q in blocked:
                value = jnp.where(value != value, relaxed[turn, PLACE[OPPOSITE[q]], x + 1, tile], value)
            values.append(value)
        return values


def solid_tile(solid, x, tile):
    return solid[x, :, tile * LANES : (tile + 1) * LANES] == 1


def coalesce(fine, fine_turn, coarse, coarse_turn, pairs, halves):
    lane = lax.broadcasted_iota(jnp.int32, (ROWS, LANES), 1)
    for x in range(coarse.width):
        for no, q in enumerate(UPWARD):
            for tile in range(fine.tiles):
                both = (
                    fine.relaxed[fine_turn, PLACE[q], 2 * x + 1, tile]
                    + fine.relaxed[fine_turn, PLACE[q], 2 * x + 2, tile]
                )
                both = both + pltpu.roll(both, 1, 0)
                pairs[tile, pl.ds(5 * x + no, 1), :] = both[ROWS - 1 : ROWS, :]
    for block in range((5 * coarse.width + ROWS - 1) // ROWS):
        rows = pl.ds(block * ROWS, ROWS)
        packed = []
        for tile in range(fine.tiles):
            value = pairs[tile, rows, :]
            value = (value + pltpu.roll(value, LANES - 1, 1)) * 0.125
            for bit in range(6):
                shifted = pltpu.roll(value, LANES - 2**bit, 1)
                value = jnp.where((lane & 2**bit) != 0, shifted, value)
            packed.append(value)
        for tile in range(coarse.tiles):
            upper = pltpu.roll(packed[2 * tile + 1], LANES // 2, 1)
            halves[tile, rows, :] = jnp.where(lane < LANES // 2, packed[2 * tile], upper)
    for x in range(coarse.width):
        for no in range(5):
            for tile in range(coarse.tiles):
                coarse.sent[coarse_turn, 0, x + 1, pl.ds(no * coarse.tiles + tile, 1), :] = halves[
                    tile, pl.ds(5 * x + no, 1), :
                ]


def explode(coarse, coarse_turn, target, fine, pairs, halves):
    lane = lax.broadcasted_iota(jnp.int32, (ROWS, LANES), 1)
    for x in range(coarse.width):
        for no, q in enumerate(DOWNWARD):
            for tile in range(coarse.tiles):
                halves[tile, pl.ds(5 * x + no, 1), :] = coarse.relaxed[
                    coarse_turn, PLACE[q], x + 1, tile, pl.ds(0, 1), :
                ]
    for block in range((5 * coarse.width + ROWS - 1) // ROWS):
        rows = pl.ds(block * ROWS, ROWS)
        for tile in range(fine.tiles):
            value = halves[tile // 2, rows, :]
            if tile % 2 == 1:
                value = pltpu.roll(value, LANES // 2, 1)
            for bit in range(5, -1, -1):
                shifted = pltpu.roll(value, 2**bit, 1)
                value = jnp.where((lane & 2 ** (bit + 1)) != 0, shifted, value)
            value = jnp.where((lane & 1) != 0, pltpu.roll(value, 1, 1), value)
            pairs[tile, rows, :] = value
    for x in range(fine.width):
        for no in range(5):
            for tile in range(fine.tiles):
                target[x + 1, pl.ds(no * fine.tiles + tile, 1), :] = pairs[
                    tile, pl.ds(5 * (x // 2) + no, 1), :
                ]


def kernel(
    sizes,
    coarse_in,
    medium_in,
    fine_in,
    solid_in,
    shear_ref,
    coarse_own,
    medium_own,
    fine_own,
    solid_own,
    fine_relaxed,
    fine_came,
    pairs,
    halves,
    exploded,
    own_sem,
    *rest,
):
    coarse = Level(1, 1, *rest[:5])
    medium = Level(2, 2, *rest[5:10])
    fine = Level(4, 4, fine_relaxed, rest[10], fine_came, *rest[11:])
    curve_size, level_size = sizes
    me_x, me_y = lax.axis_index("curve"), lax.axis_index("level")
    left, right = lax.rem(me_x + curve_size - 1, curve_size), lax.rem(me_x + 1, curve_size)
    below, above = lax.rem(me_y + level_size - 1, level_size), lax.rem(me_y + 1, level_size)
    around = ((left, right), (below, above), (me_x, me_y))
    at_bottom = me_y == 0
    at_top = me_y == level_size - 1

    def plane_load(x):
        return pltpu.make_async_copy(fine_in.at[:, pl.ds(x, 1)], fine_own.at[:, pl.ds(x, 1)], own_sem.at[x])

    solid_load = pltpu.make_async_copy(solid_in, solid_own, own_sem.at[4])
    medium_load = pltpu.make_async_copy(medium_in, medium_own, own_sem.at[5])
    coarse_load = pltpu.make_async_copy(coarse_in, coarse_own, own_sem.at[6])
    medium_load.start()
    for x in (0, 3):
        plane_load(x).start()
    solid_load.start()
    for x in (1, 2):
        plane_load(x).start()
    coarse_load.start()

    barrier = pltpu.get_barrier_semaphore()
    for device in (
        (left, me_y),
        (right, me_y),
        (me_x, below),
        (me_x, above),
        (left, below),
        (left, above),
        (right, below),
        (right, above),
    ):
        pl.semaphore_signal(barrier, inc=1, device_id=device, device_id_type=pl.DeviceIdType.MESH)

    shear = jnp.broadcast_to(shear_ref[...], (ROWS, LANES))
    excess = 1.0 / shear - 0.5
    rates = [1.0 / (2.0**t * excess + 0.5) for t in range(3)]

    def taken(own, x, tile):
        return [own[q, x, :, tile * LANES : (tile + 1) * LANES] for q in range(19)]

    def sweep(level, body):
        def plane(x, carry):
            for tile in range(level.tiles):
                body(x, tile)
            return carry

        if level.width == 1:
            plane(0, 0)
        else:
            lax.fori_loop(0, level.width, plane, 0)

    def put(level, own, turn, blocked):
        def body(x, tile):
            values = level.streamed(turn, x, tile, blocked)
            for q in range(19):
                own[q, x, :, tile * LANES : (tile + 1) * LANES] = values[q]

        return body

    def send(level, turn, which):
        copies = level.copies(turn, around)
        for no in which:
            copies[no]().start()

    def receive(level, turn, which=CORNERS_FIRST):
        copies = level.copies(turn, around)
        for no in which:
            copies[no]().wait_recv()

    def sent_off(level, turn):
        for copy in level.copies(turn, around):
            copy().wait_send()

    def wall_above(turn, x):
        fine.sent[turn, 0, x + 1] = jnp.full(fine.sent.shape[3:], SOLID, jnp.float32)

    def edges(turn, x):
        @pl.when(at_top)
        def _():
            wall_above(turn, x)

        @pl.when(at_bottom)
        def _():
            fine.sent[turn, 1, x + 1] = exploded[x + 1]

    def fine_pass(turn, relax):
        def plane(x):
            relax(x)
            edges(turn, x)

        if turn > 0:
            receive(fine, turn - 1, ROWS_ONLY + FROM_LEFT)
        plane(0)
        if turn == 0:
            pl.semaphore_wait(barrier, 8)
        send(fine, turn, FROM_RIGHT)
        if turn > 0:
            receive(fine, turn - 1, FROM_RIGHT)
        plane(3)
        send(fine, turn, FROM_LEFT)

        def inner(x, carry):
            plane(x)
            return carry

        lax.fori_loop(1, 3, inner, 0)
        send(fine, turn, ROWS_ONLY)

    medium_load.wait()
    sweep(medium, lambda x, tile: medium.keep(0, x, tile, collide(taken(medium_own, x, tile), rates[1], None)))

    @pl.when(at_bottom)
    def _():
        explode(medium, 0, exploded, fine, pairs, halves)

    solid_load.wait()

    def first(x):
        plane_load(x).wait()
        for tile in range(fine.tiles):
            fine.keep(0, x, tile, collide(taken(fine_own, x, tile), rates[2], solid_tile(solid_own, x, tile)))

    fine_pass(0, first)
    coarse_load.wait()
    sweep(coarse, lambda x, tile: coarse.keep(0, x, tile, collide(taken(coarse_own, x, tile), rates[0], None)))

    @pl.when(at_top)
    def _():
        coalesce(fine, 0, medium, 0, pairs, halves)
        coalesce(medium, 0, coarse, 0, pairs, halves)

    @pl.when(at_bottom)
    def _():
        coarse.sent[0, 1] = jnp.full(coarse.sent.shape[2:], SOLID, jnp.float32)
        explode(coarse, 0, medium.sent.at[0, 1], medium, pairs, halves)

    send(medium, 0, CORNERS_FIRST)
    send(coarse, 0, CORNERS_FIRST)

    def again(turn):
        def relax(x):
            for tile in range(fine.tiles):
                values = fine.streamed(turn - 1, x, tile, EVERY)
                fine.keep(turn, x, tile, collide(values, rates[2], solid_tile(solid_own, x, tile)))

        fine_pass(turn, relax)

    again(1)
    receive(medium, 0)
    sweep(
        medium,
        lambda x, tile: medium.keep(1, x, tile, collide(medium.streamed(0, x, tile, ()), rates[1], None)),
    )

    @pl.when(at_bottom)
    def _():
        explode(medium, 1, exploded, fine, pairs, halves)
        medium.sent[1, 1] = medium.sent[0, 1]

    receive(coarse, 0)
    sweep(coarse, put(coarse, coarse_own, 0, DOWNWARD))

    again(2)

    @pl.when(at_top)
    def _():
        coalesce(fine, 2, medium, 1, pairs, halves)

    send(medium, 1, CORNERS_FIRST)

    again(3)
    receive(medium, 1)
    sweep(medium, put(medium, medium_own, 1, ()))
    sent_off(coarse, 0)
    sent_off(medium, 0)
    sent_off(medium, 1)
    for turn in range(SUBSTEPS - 1):
        sent_off(fine, turn)

    receive(fine, SUBSTEPS - 1, ROWS_ONLY)

    def inner(x, carry):
        for tile in range(fine.tiles):
            values = fine.streamed(SUBSTEPS - 1, x, tile, EVERY)
            lanes = slice(tile * LANES, (tile + 1) * LANES)
            solid = solid_tile(solid_own, x, tile)
            for q in range(19):
                fine_own[q, x, :, lanes] = jnp.where(solid, fine_own[q, x, :, lanes], values[q])
        return carry

    lax.fori_loop(1, 3, inner, 0)
    receive(fine, SUBSTEPS - 1, FROM_LEFT + FROM_RIGHT)
    sent_off(fine, SUBSTEPS - 1)


def finish(coarse, medium, inner, fine_relaxed, fine_came, coarse_out, medium_out, fine_out, outer, sem):
    planes = pl.ds(1, 2)
    done = [
        pltpu.make_async_copy(source, target, sem.at[no])
        for no, (source, target) in enumerate(
            ((inner.at[:, planes], fine_out.at[:, planes]), (medium, medium_out), (coarse, coarse_out))
        )
    ]
    for copy in done:
        copy.start()
    fine = Level(4, 4, fine_relaxed, None, fine_came, None, None)
    for no, x in enumerate((0, 3)):
        for tile in range(fine.tiles):
            values = fine.streamed(SUBSTEPS - 1, x, tile, EVERY)
            for q in range(19):
                outer[q, no, :, tile * LANES : (tile + 1) * LANES] = values[q]
        store = pltpu.make_async_copy(outer.at[:, pl.ds(no, 1)], fine_out.at[:, pl.ds(x, 1)], sem.at[3 + no])
        store.start()
        done.append(store)
    for copy in done:
        copy.wait()


def shards(coarse_pops, medium_pops, fine_pops, solid_cells, shear_rate):
    sizes = (lax.axis_size("curve"), lax.axis_size("level"))
    scratch = [
        pltpu.VMEM((4, 16, LANES), jnp.float32),
        pltpu.VMEM((2, 16, LANES), jnp.float32),
        pltpu.VMEM((6, 24, LANES), jnp.float32),
        pltpu.SemaphoreType.DMA((7,)),
    ]
    for t, turns in ((0, 1), (1, 2), (2, SUBSTEPS)):
        width = tiles = 2**t
        lines = (5 * tiles + ROWS - 1) // ROWS * ROWS
        relaxed = pltpu.VMEM((turns, 19, width + 2, tiles, ROWS, LANES), jnp.float32)
        edge_rows = pltpu.VMEM((turns, 2, width + 2, lines, LANES), jnp.float32)
        scratch += [edge_rows] if t == 2 else [relaxed, edge_rows, edge_rows]
        scratch += [pltpu.SemaphoreType.DMA((turns, 8))] * 2
    given = (coarse_pops, medium_pops, fine_pops, solid_cells)
    in_vmem = pl.BlockSpec(memory_space=pltpu.VMEM)
    held = pl.pallas_call(
        lambda *refs: kernel(sizes, *refs),
        out_shape=tuple(pltpu.VMEM(array.shape, array.dtype) for array in given) + (relaxed, edge_rows),
        in_specs=[pl.BlockSpec(memory_space=pltpu.HBM)] * 4 + [in_vmem],
        out_specs=(in_vmem,) * 6,
        scratch_shapes=scratch,
        compiler_params=pltpu.CompilerParams(
            collective_id=0, has_side_effects=True, vmem_limit_bytes=24 * 1024 * 1024
        ),
    )(*[pltpu.with_memory_space_constraint(array, pltpu.HBM) for array in given], shear_rate)
    return pl.pallas_call(
        finish,
        out_shape=tuple(jax.ShapeDtypeStruct(pops.shape, jnp.float32) for pops in given[:3]),
        in_specs=[in_vmem] * 5,
        out_specs=(pl.BlockSpec(memory_space=pl.ANY),) * 3,
        scratch_shapes=[pltpu.VMEM((19, 2, ROWS, 4 * LANES), jnp.float32), pltpu.SemaphoreType.DMA((5,))],
        compiler_params=pltpu.CompilerParams(vmem_limit_bytes=24 * 1024 * 1024),
    )(*held[:3], *held[4:])


def solution(mesh):
    lattice = P(None, "curve", "level", None)
    return jax.shard_map(
        shards,
        mesh=mesh,
        in_specs=(lattice, lattice, lattice, P("curve", "level", None), P("curve", "level")),
        out_specs=(lattice, lattice, lattice),
        check_vma=False,
    )
```

```python
import jax
import jax.numpy as jnp
from jax import lax
from jax.experimental import pallas as pl
from jax.experimental.pallas import tpu as pltpu
from jax.sharding import PartitionSpec as P

VELOCITIES = [
    (0, 0, 0),
    (1, 0, 0),
    (-1, 0, 0),
    (0, 1, 0),
    (0, -1, 0),
    (0, 0, 1),
    (0, 0, -1),
    (1, 1, 0),
    (-1, -1, 0),
    (1, -1, 0),
    (-1, 1, 0),
    (1, 0, 1),
    (-1, 0, -1),
    (1, 0, -1),
    (-1, 0, 1),
    (0, 1, 1),
    (0, -1, -1),
    (0, 1, -1),
    (0, -1, 1),
]
OPPOSITE = [0, 2, 1, 4, 3, 6, 5, 8, 7, 10, 9, 12, 11, 14, 13, 16, 15, 18, 17]

ORDER = [1, 7, 9, 11, 13, 2, 8, 10, 12, 14, 0, 3, 4, 5, 6, 15, 16, 17, 18]
PLACE = [ORDER.index(q) for q in range(19)]
UPWARD = [7, 3, 10, 15, 17]
DOWNWARD = [9, 4, 8, 16, 18]
ROWS = 8
LANES = 128
SUBSTEPS = 4
EVERY = tuple(range(1, 19))
FROM_LEFT = (4, 5, 0)
FROM_RIGHT = (6, 7, 1)
ROWS_ONLY = (2, 3)
ROWS_0 = (8, 9)
ROWS_3 = (10, 11)
CORNERS_FIRST = (4, 5, 6, 7, 0, 1, 2, 3)
SOLID = float("nan")


def collide(f, rate, solid):
    s = {}
    d = {}
    for q in (1, 3, 5, 7, 9, 11, 13, 15, 17):
        s[q] = f[q] + f[q + 1]
        d[q] = f[q] - f[q + 1]
    xy, xz, yz = s[7] + s[9], s[11] + s[13], s[15] + s[17]
    pxy, pxz, pyz = s[7] - s[9], s[11] - s[13], s[15] - s[17]
    axis_sum = s[1] + s[3] + s[5]
    edge_sum = xy + xz + yz
    density = f[0] + axis_sum + edge_sum
    if solid is not None:
        density = jnp.where(solid, SOLID, density)
    inverse = 1.0 / density
    x_xy, y_xy = d[7] + d[9], d[7] - d[9]
    x_xz, z_xz = d[11] + d[13], d[11] - d[13]
    y_yz, z_yz = d[15] + d[17], d[15] - d[17]
    sum_x, sum_y, sum_z = x_xy + x_xz, y_xy + y_yz, z_xz + z_yz
    jx, jy, jz = d[1] + sum_x, d[3] + sum_y, d[5] + sum_z
    ux, uy, uz = jx * inverse, jy * inverse, jz * inverse
    xx, yy, zz = jx * ux, jy * uy, jz * uz
    yy_zz = yy + zz
    energy = xx + yy_zz

    tx, ty, tz = sum_x - 2.0 * d[1], sum_y - 2.0 * d[3], sum_z - 2.0 * d[5]
    mx = 0.2475 * (x_xy - x_xz)
    my = 0.2475 * (y_yz - y_xy)
    mz = 0.2475 * (z_xz - z_yz)
    hx, hy, hz = 0.05 * tx, 0.05 * ty, 0.05 * tz
    ax, ay, az = 0.2 * tx, 0.2 * ty, 0.2 * tz
    x1, x2 = hx + mx, hx - mx
    y1, y2 = hy - my, hy + my
    z1, z2 = hz + mz, hz - mz

    alpha = (1.19 * 19.0 / 2394.0) * (edge_sum - f[0] - energy)
    beta = (1.4 / 252.0) * (9.0 * f[0] - 7.0 * axis_sum - 2.0 * edge_sum + 5.5 * energy)
    base0 = 30.0 * alpha - 12.0 * beta
    base1 = 11.0 * alpha + 4.0 * beta
    base2 = 8.0 * alpha + beta
    u1 = 3.0 * s[1] - axis_sum
    u2 = edge_sum - 3.0 * yz
    pxx = 2.0 * xx - yy_zz
    gamma = (rate * (1.0 / 36.0)) * (u1 + u2 - pxx)
    delta = (1.4 / 72.0) * (u2 - 2.0 * u1 + 0.5 * pxx)
    v1 = s[3] - s[5]
    v2 = xy - xz
    ww = yy - zz
    eps = (rate * (1.0 / 12.0)) * (v1 + v2 - ww)
    zeta = (1.4 / 24.0) * (v2 - 2.0 * v1 + 0.5 * ww)
    g1, g2 = gamma - 2.0 * delta, gamma + delta
    h1, h2 = eps - 2.0 * zeta, eps + zeta
    quarter = rate * 0.25
    nxy = quarter * (pxy - jx * uy)
    nxz = quarter * (pxz - jx * uz)
    nyz = quarter * (pyz - jy * uz)
    ex = base1 - 2.0 * g1
    eyz = base1 + g1
    ey, ez = eyz - h1, eyz + h1
    low = base2 + g2
    exy, exz = low + h2, low - h2
    eyz2 = base2 - 2.0 * g2
    out = [None] * 19
    out[0] = f[0] + base0
    for q, even, odd in ((1, ex, ax), (3, ey, ay), (5, ez, az)):
        out[q] = f[q] + (even + odd)
        out[q + 1] = f[q + 1] + (even - odd)
    for q, even, odd in (
        (7, exy + nxy, x1 + y1),
        (9, exy - nxy, x1 - y1),
        (11, exz + nxz, x2 + z1),
        (13, exz - nxz, x2 - z1),
        (15, eyz2 + nyz, y2 + z2),
        (17, eyz2 - nyz, y2 - z2),
    ):
        out[q] = f[q] - (even + odd)
        out[q + 1] = f[q + 1] - (even - odd)
    return out


class Level:
    def __init__(self, width, tiles, relaxed, sent, came, send_sem, recv_sem):
        self.width, self.tiles = width, tiles
        self.relaxed, self.sent, self.came = relaxed, sent, came
        self.send_sem, self.recv_sem = send_sem, recv_sem

    def copies(self, turn, around):
        width, tiles = self.width, self.tiles
        third = (2 * tiles // ROWS) * ROWS
        relaxed, sent, came = self.relaxed, self.sent, self.came
        (left, right), (below, above), (me_x, me_y) = around

        def copy(no, source, target, device):
            return lambda: pltpu.make_async_remote_copy(
                src_ref=source,
                dst_ref=target,
                send_sem=self.send_sem.at[turn, no],
                recv_sem=self.recv_sem.at[turn, no],
                device_id=device,
                device_id_type=pl.DeviceIdType.MESH,
            )

        groups = [pl.ds(1, width)] if width < 4 else [pl.ds(2, 2), pl.ds(1, 1), pl.ds(4, 1)]
        rows = groups[0]
        first, last = pl.ds(0, ROWS), pl.ds(third, ROWS)
        result = [
            copy(0, relaxed.at[turn, pl.ds(0, 5), width], relaxed.at[turn, pl.ds(0, 5), 0], (right, me_y)),
            copy(1, relaxed.at[turn, pl.ds(5, 5), 1], relaxed.at[turn, pl.ds(5, 5), width + 1], (left, me_y)),
        ]
        for way, beyond in ((0, above), (1, below)):
            result.append(copy(2 + way, sent.at[turn, way, rows], came.at[turn, way, rows], (me_x, beyond)))
        for way, beyond in ((0, above), (1, below)):
            result.append(
                copy(4 + way, sent.at[turn, way, width, first], came.at[turn, way, 0, first], (right, beyond))
            )
        for way, beyond in ((0, above), (1, below)):
            result.append(
                copy(6 + way, sent.at[turn, way, 1, last], came.at[turn, way, width + 1, last], (left, beyond))
            )
        for no, group in enumerate(groups[1:]):
            for way, beyond in ((0, above), (1, below)):
                result.append(
                    copy(8 + 2 * no + way, sent.at[turn, way, group], came.at[turn, way, group], (me_x, beyond))
                )
        return result

    def keep(self, turn, x, tile, values):
        for q in range(19):
            self.relaxed[turn, PLACE[q], x + 1, tile] = values[q]
        for way, group, row in ((0, UPWARD, ROWS - 1), (1, DOWNWARD, 0)):
            for no, q in enumerate(group):
                self.sent[turn, way, x + 1, pl.ds(no * self.tiles + tile, 1), :] = values[q][row : row + 1, :]

    def streamed(self, turn, x, tile, blocked):
        lane = lax.broadcasted_iota(jnp.int32, (ROWS, LANES), 1)
        row = lax.broadcasted_iota(jnp.int32, (ROWS, LANES), 0)
        relaxed, came, tiles = self.relaxed, self.came, self.tiles
        values = []
        for q, (step_x, step_y, step_z) in enumerate(VELOCITIES):
            plane = x + 1 - step_x
            place = PLACE[q]
            value = relaxed[turn, place, plane, tile]
            beside = (tile - step_z) % tiles
            crossing = lane == (LANES - 1 if step_z > 0 else 0)
            if step_z != 0 and tiles > 1:
                value = jnp.where(crossing, relaxed[turn, place, plane, beside], value)
            if step_y != 0:
                way = 0 if step_y > 0 else 1
                no = (UPWARD if step_y > 0 else DOWNWARD).index(q) * tiles

                def ghost(at):
                    line = came[turn, way, plane, pl.ds(no + at, 1), :]
                    return jnp.broadcast_to(line, (ROWS, LANES))

                edge = ghost(tile)
                if step_z != 0 and tiles > 1:
                    edge = jnp.where(crossing, ghost(beside), edge)
                value = pltpu.roll(value, 1 if step_y > 0 else ROWS - 1, 0)
                value = jnp.where(row == (0 if step_y > 0 else ROWS - 1), edge, value)
            if step_z != 0:
                value = pltpu.roll(value, 1 if step_z > 0 else LANES - 1, 1)
            if q in blocked:
                value = jnp.where(value != value, relaxed[turn, PLACE[OPPOSITE[q]], x + 1, tile], value)
            values.append(value)
        return values


def solid_tile(solid, x, tile):
    return solid[x, :, tile * LANES : (tile + 1) * LANES] == 1


def coalesce(fine, fine_turn, coarse, coarse_turn, pairs, halves):
    lane = lax.broadcasted_iota(jnp.int32, (ROWS, LANES), 1)
    for x in range(coarse.width):
        for no, q in enumerate(UPWARD):
            for tile in range(fine.tiles):
                both = (
                    fine.relaxed[fine_turn, PLACE[q], 2 * x + 1, tile]
                    + fine.relaxed[fine_turn, PLACE[q], 2 * x + 2, tile]
                )
                both = both + pltpu.roll(both, 1, 0)
                pairs[tile, pl.ds(5 * x + no, 1), :] = both[ROWS - 1 : ROWS, :]
    for block in range((5 * coarse.width + ROWS - 1) // ROWS):
        rows = pl.ds(block * ROWS, ROWS)
        packed = []
        for tile in range(fine.tiles):
            value = pairs[tile, rows, :]
            value = (value + pltpu.roll(value, LANES - 1, 1)) * 0.125
            for bit in range(6):
                shifted = pltpu.roll(value, LANES - 2**bit, 1)
                value = jnp.where((lane & 2**bit) != 0, shifted, value)
            packed.append(value)
        for tile in range(coarse.tiles):
            upper = pltpu.roll(packed[2 * tile + 1], LANES // 2, 1)
            halves[tile, rows, :] = jnp.where(lane < LANES // 2, packed[2 * tile], upper)
    for x in range(coarse.width):
        for no in range(5):
            for tile in range(coarse.tiles):
                coarse.sent[coarse_turn, 0, x + 1, pl.ds(no * coarse.tiles + tile, 1), :] = halves[
                    tile, pl.ds(5 * x + no, 1), :
                ]


def explode(coarse, coarse_turn, target, fine, pairs, halves):
    lane = lax.broadcasted_iota(jnp.int32, (ROWS, LANES), 1)
    for x in range(coarse.width):
        for no, q in enumerate(DOWNWARD):
            for tile in range(coarse.tiles):
                halves[tile, pl.ds(5 * x + no, 1), :] = coarse.relaxed[
                    coarse_turn, PLACE[q], x + 1, tile, pl.ds(0, 1), :
                ]
    for block in range((5 * coarse.width + ROWS - 1) // ROWS):
        rows = pl.ds(block * ROWS, ROWS)
        for tile in range(fine.tiles):
            value = halves[tile // 2, rows, :]
            if tile % 2 == 1:
                value = pltpu.roll(value, LANES // 2, 1)
            for bit in range(5, -1, -1):
                shifted = pltpu.roll(value, 2**bit, 1)
                value = jnp.where((lane & 2 ** (bit + 1)) != 0, shifted, value)
            value = jnp.where((lane & 1) != 0, pltpu.roll(value, 1, 1), value)
            pairs[tile, rows, :] = value
    for x in range(fine.width):
        for no in range(5):
            for tile in range(fine.tiles):
                target[x + 1, pl.ds(no * fine.tiles + tile, 1), :] = pairs[
                    tile, pl.ds(5 * (x // 2) + no, 1), :
                ]


def kernel(
    sizes,
    coarse_in,
    medium_in,
    fine_in,
    solid_in,
    shear_ref,
    coarse_own,
    medium_own,
    fine_own,
    solid_own,
    fine_relaxed,
    fine_came,
    pairs,
    halves,
    exploded,
    own_sem,
    *rest,
):
    coarse = Level(1, 1, *rest[:5])
    medium = Level(2, 2, *rest[5:10])
    fine = Level(4, 4, fine_relaxed, rest[10], fine_came, *rest[11:])
    curve_size, level_size = sizes
    me_x, me_y = lax.axis_index("curve"), lax.axis_index("level")
    left, right = lax.rem(me_x + curve_size - 1, curve_size), lax.rem(me_x + 1, curve_size)
    below, above = lax.rem(me_y + level_size - 1, level_size), lax.rem(me_y + 1, level_size)
    around = ((left, right), (below, above), (me_x, me_y))
    at_bottom = me_y == 0
    at_top = me_y == level_size - 1

    def plane_load(x):
        return pltpu.make_async_copy(fine_in.at[:, pl.ds(x, 1)], fine_own.at[:, pl.ds(x, 1)], own_sem.at[x])

    solid_load = pltpu.make_async_copy(solid_in, solid_own, own_sem.at[4])
    medium_load = pltpu.make_async_copy(medium_in, medium_own, own_sem.at[5])
    coarse_load = pltpu.make_async_copy(coarse_in, coarse_own, own_sem.at[6])
    barrier = pltpu.get_barrier_semaphore()
    for device in (
        (left, below),
        (left, above),
        (right, below),
        (right, above),
        (left, me_y),
        (right, me_y),
        (me_x, below),
        (me_x, above),
    ):
        pl.semaphore_signal(barrier, inc=1, device_id=device, device_id_type=pl.DeviceIdType.MESH)

    medium_load.start()
    for x in (0, 3):
        plane_load(x).start()
    solid_load.start()
    for x in (1, 2):
        plane_load(x).start()
    coarse_load.start()

    shear = jnp.broadcast_to(shear_ref[...], (ROWS, LANES))
    excess = 1.0 / shear - 0.5
    rates = [1.0 / (2.0**t * excess + 0.5) for t in range(3)]

    def taken(own, x, tile):
        return [own[q, x, :, tile * LANES : (tile + 1) * LANES] for q in range(19)]

    def sweep(level, body):
        def plane(x, carry):
            for tile in range(level.tiles):
                body(x, tile)
            return carry

        if level.width == 1:
            plane(0, 0)
        else:
            lax.fori_loop(0, level.width, plane, 0)

    def put(level, own, turn, blocked):
        def body(x, tile):
            values = level.streamed(turn, x, tile, blocked)
            for q in range(19):
                own[q, x, :, tile * LANES : (tile + 1) * LANES] = values[q]

        return body

    def send(level, turn, which):
        copies = level.copies(turn, around)
        for no in which:
            copies[no]().start()

    def receive(level, turn, which=CORNERS_FIRST):
        copies = level.copies(turn, around)
        for no in which:
            copies[no]().wait_recv()

    def sent_off(level, turn):
        for copy in level.copies(turn, around):
            copy().wait_send()

    def wall_above(turn, x):
        fine.sent[turn, 0, x + 1] = jnp.full(fine.sent.shape[3:], SOLID, jnp.float32)

    def edges(turn, x):
        @pl.when(at_top)
        def _():
            wall_above(turn, x)

        @pl.when(at_bottom)
        def _():
            fine.sent[turn, 1, x + 1] = exploded[x + 1]

    def fine_pass(turn, relax):
        def plane(x):
            relax(x)
            edges(turn, x)

        if turn > 0:
            receive(fine, turn - 1, ROWS_0 + ROWS_3 + ROWS_ONLY + FROM_LEFT)
        plane(0)
        if turn > 0:
            send(fine, turn, FROM_RIGHT + ROWS_0)
            receive(fine, turn - 1, FROM_RIGHT)
        plane(3)
        if turn > 0:
            send(fine, turn, FROM_LEFT + ROWS_3)

        def inner(x, carry):
            plane(x)
            return carry

        lax.fori_loop(1, 3, inner, 0)
        if turn > 0:
            send(fine, turn, ROWS_ONLY)

    medium_load.wait()
    sweep(medium, lambda x, tile: medium.keep(0, x, tile, collide(taken(medium_own, x, tile), rates[1], None)))

    @pl.when(at_bottom)
    def _():
        explode(medium, 0, exploded, fine, pairs, halves)

    solid_load.wait()

    def first(x):
        plane_load(x).wait()
        for tile in range(fine.tiles):
            fine.keep(0, x, tile, collide(taken(fine_own, x, tile), rates[2], solid_tile(solid_own, x, tile)))

    fine_pass(0, first)
    pl.semaphore_wait(barrier, 8)
    send(fine, 0, CORNERS_FIRST + ROWS_0 + ROWS_3)
    coarse_load.wait()
    sweep(coarse, lambda x, tile: coarse.keep(0, x, tile, collide(taken(coarse_own, x, tile), rates[0], None)))

    @pl.when(at_top)
    def _():
        coalesce(fine, 0, medium, 0, pairs, halves)
        coalesce(medium, 0, coarse, 0, pairs, halves)

    @pl.when(at_bottom)
    def _():
        coarse.sent[0, 1] = jnp.full(coarse.sent.shape[2:], SOLID, jnp.float32)
        explode(coarse, 0, medium.sent.at[0, 1], medium, pairs, halves)

    send(medium, 0, CORNERS_FIRST)
    send(coarse, 0, CORNERS_FIRST)

    def again(turn):
        def relax(x):
            for tile in range(fine.tiles):
                values = fine.streamed(turn - 1, x, tile, EVERY)
                fine.keep(turn, x, tile, collide(values, rates[2], solid_tile(solid_own, x, tile)))

        fine_pass(turn, relax)

    again(1)
    receive(medium, 0)
    sweep(
        medium,
        lambda x, tile: medium.keep(1, x, tile, collide(medium.streamed(0, x, tile, ()), rates[1], None)),
    )

    @pl.when(at_bottom)
    def _():
        explode(medium, 1, exploded, fine, pairs, halves)
        medium.sent[1, 1] = medium.sent[0, 1]

    receive(coarse, 0)
    sweep(coarse, put(coarse, coarse_own, 0, DOWNWARD))

    again(2)

    @pl.when(at_top)
    def _():
        coalesce(fine, 2, medium, 1, pairs, halves)

    send(medium, 1, CORNERS_FIRST)

    again(3)
    receive(medium, 1)
    sweep(medium, put(medium, medium_own, 1, ()))
    sent_off(coarse, 0)
    sent_off(medium, 0)
    sent_off(medium, 1)
    for turn in range(SUBSTEPS - 1):
        sent_off(fine, turn)

    receive(fine, SUBSTEPS - 1, ROWS_0 + ROWS_3 + ROWS_ONLY)

    def inner(x, carry):
        for tile in range(fine.tiles):
            values = fine.streamed(SUBSTEPS - 1, x, tile, EVERY)
            lanes = slice(tile * LANES, (tile + 1) * LANES)
            solid = solid_tile(solid_own, x, tile)
            for q in range(19):
                fine_own[q, x, :, lanes] = jnp.where(solid, fine_own[q, x, :, lanes], values[q])
        return carry

    lax.fori_loop(1, 3, inner, 0)
    receive(fine, SUBSTEPS - 1, FROM_LEFT + FROM_RIGHT)
    sent_off(fine, SUBSTEPS - 1)


def finish(coarse, medium, inner, fine_relaxed, fine_came, coarse_out, medium_out, fine_out, outer, sem):
    planes = pl.ds(1, 2)
    done = [
        pltpu.make_async_copy(source, target, sem.at[no])
        for no, (source, target) in enumerate(
            ((inner.at[:, planes], fine_out.at[:, planes]), (medium, medium_out), (coarse, coarse_out))
        )
    ]
    for copy in done:
        copy.start()
    fine = Level(4, 4, fine_relaxed, None, fine_came, None, None)
    for no, x in enumerate((0, 3)):
        for tile in range(fine.tiles):
            values = fine.streamed(SUBSTEPS - 1, x, tile, EVERY)
            for q in range(19):
                outer[q, no, :, tile * LANES : (tile + 1) * LANES] = values[q]
        store = pltpu.make_async_copy(outer.at[:, pl.ds(no, 1)], fine_out.at[:, pl.ds(x, 1)], sem.at[3 + no])
        store.start()
        done.append(store)
    for copy in done:
        copy.wait()


def shards(coarse_pops, medium_pops, fine_pops, solid_cells, shear_rate):
    sizes = (lax.axis_size("curve"), lax.axis_size("level"))
    scratch = [
        pltpu.VMEM((4, 16, LANES), jnp.float32),
        pltpu.VMEM((2, 16, LANES), jnp.float32),
        pltpu.VMEM((6, 24, LANES), jnp.float32),
        pltpu.SemaphoreType.DMA((7,)),
    ]
    for t, turns in ((0, 1), (1, 2), (2, SUBSTEPS)):
        width = tiles = 2**t
        lines = (5 * tiles + ROWS - 1) // ROWS * ROWS
        relaxed = pltpu.VMEM((turns, 19, width + 2, tiles, ROWS, LANES), jnp.float32)
        edge_rows = pltpu.VMEM((turns, 2, width + 2, lines, LANES), jnp.float32)
        scratch += [edge_rows] if t == 2 else [relaxed, edge_rows, edge_rows]
        scratch += [pltpu.SemaphoreType.DMA((turns, 12 if t == 2 else 8))] * 2
    given = (coarse_pops, medium_pops, fine_pops, solid_cells)
    in_vmem = pl.BlockSpec(memory_space=pltpu.VMEM)
    held = pl.pallas_call(
        lambda *refs: kernel(sizes, *refs),
        out_shape=tuple(pltpu.VMEM(array.shape, array.dtype) for array in given) + (relaxed, edge_rows),
        in_specs=[pl.BlockSpec(memory_space=pltpu.HBM)] * 4 + [in_vmem],
        out_specs=(in_vmem,) * 6,
        scratch_shapes=scratch,
        compiler_params=pltpu.CompilerParams(
            collective_id=0, has_side_effects=True, vmem_limit_bytes=24 * 1024 * 1024
        ),
    )(*[pltpu.with_memory_space_constraint(array, pltpu.HBM) for array in given], shear_rate)
    return pl.pallas_call(
        finish,
        out_shape=tuple(jax.ShapeDtypeStruct(pops.shape, jnp.float32) for pops in given[:3]),
        in_specs=[in_vmem] * 5,
        out_specs=(pl.BlockSpec(memory_space=pl.ANY),) * 3,
        scratch_shapes=[pltpu.VMEM((19, 2, ROWS, 4 * LANES), jnp.float32), pltpu.SemaphoreType.DMA((5,))],
        compiler_params=pltpu.CompilerParams(vmem_limit_bytes=24 * 1024 * 1024),
    )(*held[:3], *held[4:])


def solution(mesh):
    lattice = P(None, "curve", "level", None)
    return jax.shard_map(
        shards,
        mesh=mesh,
        in_specs=(lattice, lattice, lattice, P("curve", "level", None), P("curve", "level")),
        out_specs=(lattice, lattice, lattice),
        check_vma=False,
    )
```
